32 devices in a mesh: dir: 2 (over x), gx: 16 (over z, y, core).
Axes of the slice: x: 2, y: 2, z: 4, core: 2. Of those that a mesh axis runs over, the one named last changes fastest.
Arguments:
- pops: float32 [19, 128, 64, 128], P(None, ('dir', 'gx')), parts along dimension 1, may hold values from 0.5 to 1.5
- heights: int32 [128, 128], P(('dir', 'gx')), parts along dimension 0, may hold values from 0 to 32
Outputs:
- pops_out: float32 [19, 128, 64, 128], P(None, ('dir', 'gx')), parts along dimension 1
The draws below stay inside these ranges and needn't reach their ends.
There are 2 independent parts, one for each index of `dir`. The reference program is written for one: setup_inputs(seed, part) draws one part's arguments, and reference() takes and returns one part's arrays. A program takes and returns all parts, laid end to end along the dimension named above; each array names one. Nothing has to cross between parts.
All inputs are finite; a program needn't handle non-finite values.
Results may differ from the reference program's by a relative error of at most 0.0003.
Values sent between devices are 32-bit elements; how exact they have to be, the bound alone decides.
A program may use at most 64 MiB of HBM per device.

```python
import jax
import jax.numpy as jnp
from jax import lax

Q = 19
NY = 128
NZ = 64
STEPS = 6
NX = 64


def place_ends(drawn, own_key, smallest, high):
    longest = drawn.shape.index(max(drawn.shape))
    spots = []
    for shift in (0, 1):
        where = [jax.random.randint(jax.random.fold_in(own_key, axis), (), 0, length) for axis, length in enumerate(drawn.shape)]
        where[longest] = (where[longest] + shift) % drawn.shape[longest]
        spots.append(tuple(where))
    return drawn.at[spots[0]].set(smallest).at[spots[1]].set(high)


def shard_levels(rng, shape, shards, smallest, high):
    def one(position, parts):
        steps = jax.random.uniform(jax.random.fold_in(jax.random.fold_in(rng, 6), position), (parts,), jnp.float32, smallest / len(shards), high / len(shards))
        return jnp.repeat(jnp.exp(steps), shape[position] // parts).reshape((-1,) + (1,) * (len(shape) - position - 1))

    loudness = one(*shards[0])
    for cut in shards[1:]:
        loudness = loudness * one(*cut)
    return loudness


def setup_inputs(seed: int = 0, part: int = 0) -> dict:
    arg_keys = jax.random.split(jax.random.key(seed), 3)
    part_splits = jax.random.split(jax.random.fold_in(arg_keys[2], part), 3)
    return {
        "pops": jnp.clip(0.5 + 1.0 * jax.random.uniform(part_splits[0], (Q, NX, NZ, NY), jnp.float32) ** shard_levels(part_splits[0], (Q, NX, NZ, NY), ((1, 16),), -0.2, 0.2), 0.5, 1.5),
        "heights": place_ends(jax.random.randint(part_splits[1], (NX, NY), 0, NZ // 2 + 1), jax.random.fold_in(part_splits[1], 1), 0, (NZ // 2 + 1) - 1).astype(jnp.int32),
    }


velocity_table = [(0, 0, 0), (1, 0, 0), (-1, 0, 0), (0, 1, 0), (0, -1, 0), (0, 0, 1), (0, 0, -1),
                  (1, 1, 0), (-1, -1, 0), (1, -1, 0), (-1, 1, 0), (1, 0, 1), (-1, 0, -1), (1, 0, -1), (-1, 0, 1),
                  (0, 1, 1), (0, -1, -1), (0, 1, -1), (0, -1, 1)]
weight_table = [1.0 / 3.0] + [1.0 / 18.0] * 6 + [1.0 / 36.0] * 12
omega_rate = 1.9


def opposite(component):
    if component == 0:
        return 0
    return component + 1 if component % 2 == 1 else component - 1


def collide(populations):
    density = jnp.zeros_like(populations[0])
    moment_x = jnp.zeros_like(populations[0])
    moment_y = jnp.zeros_like(populations[0])
    moment_z = jnp.zeros_like(populations[0])
    for component in range(19):
        step_x, step_y, step_z = velocity_table[component]
        term = weight_table[component] * populations[component]
        density = density + term
        if step_x != 0:
            moment_x = moment_x + step_x * term
        if step_y != 0:
            moment_y = moment_y + step_y * term
        if step_z != 0:
            moment_z = moment_z + step_z * term
    speed_x = moment_x / density
    speed_y = moment_y / density
    speed_z = moment_z / density
    speed_sq = speed_x * speed_x + speed_y * speed_y + speed_z * speed_z
    result = []
    for component in range(19):
        step_x, step_y, step_z = velocity_table[component]
        along = step_x * speed_x + step_y * speed_y + step_z * speed_z
        equil = density * (1.0 + 3.0 * along + 4.5 * along * along - 1.5 * speed_sq)
        result.append(populations[component] + omega_rate * (equil - populations[component]))
    return result


def shift_cells(field, step_x, step_z, step_y, fill):
    moved = jnp.roll(field, (step_x, step_y), axis=(0, 2))
    if step_z == 1:
        moved = jnp.concatenate([jnp.full_like(moved[:, :1], fill), moved[:, :-1]], axis=1)
    elif step_z == -1:
        moved = jnp.concatenate([moved[:, 1:], jnp.full_like(moved[:, :1], fill)], axis=1)
    return moved


def reference(pops, heights):
    shape = pops.shape[1:]
    zcoord = lax.broadcasted_iota(jnp.int32, shape, 1)
    fluid = (zcoord >= heights[:, None, :]).astype(jnp.float32)
    current = [pops[component] for component in range(19)]
    for step_count in range(STEPS):
        post = collide(current)
        current = []
        for component in range(19):
            step_x, step_y, step_z = velocity_table[component]
            source_fluid = shift_cells(fluid, step_x, step_z, step_y, 0.0)
            moved = shift_cells(post[component], step_x, step_z, step_y, 0.0)
            current.append(jnp.where(source_fluid > 0.5, moved, post[opposite(component)]))
    return jnp.stack(current)
```

```python
import functools

import jax
import jax.numpy as jnp
from jax import lax
from jax.experimental import pallas as pl
from jax.experimental.pallas import tpu as pltpu
from jax.sharding import PartitionSpec as P

STEPS = 6
PAD = 8
MESH = pl.DeviceIdType.MESH

velocity_table = [
    (0, 0, 0),
    (1, 0, 0),
    (-1, 0, 0),
    (0, 1, 0),
    (0, -1, 0),
    (0, 0, 1),
    (0, 0, -1),
    (1, 1, 0),
    (-1, -1, 0),
    (1, -1, 0),
    (-1, 1, 0),
    (1, 0, 1),
    (-1, 0, -1),
    (1, 0, -1),
    (-1, 0, 1),
    (0, 1, 1),
    (0, -1, -1),
    (0, 1, -1),
    (0, -1, 1),
]
omega_rate = 1.9
held_order = [1, 7, 9, 11, 13, 2, 8, 10, 12, 14, 0, 3, 4, 5, 6, 15, 16, 17, 18]
spot = {component: place for place, component in enumerate(held_order)}
MOVING = 5


def opposite(component):
    if component == 0:
        return 0
    return component + 1 if component % 2 == 1 else component - 1


def collide(g):
    sums = {i: g[i] + g[i + 1] for i in range(1, 19, 2)}
    diffs = {i: g[i] - g[i + 1] for i in range(1, 19, 2)}
    axis_sum = sums[1] + sums[3] + sums[5]
    cross_sum = (sums[7] + sums[9]) + (sums[11] + sums[13]) + (sums[15] + sums[17])
    total = 12.0 * g[0] + 2.0 * axis_sum + cross_sum
    scale = 3.0 * omega_rate / 36.0
    nx = scale * (2.0 * diffs[1] + ((diffs[7] + diffs[9]) + (diffs[11] + diffs[13])))
    ny = scale * (2.0 * diffs[3] + ((diffs[7] - diffs[9]) + (diffs[15] + diffs[17])))
    nz = scale * (2.0 * diffs[5] + ((diffs[11] - diffs[13]) + (diffs[15] - diffs[17])))
    k = (omega_rate * 4.5 / 36.0 / (scale * scale)) / total
    base = (omega_rate / 36.0) * total - (k * (1.0 / 3.0)) * (nx * nx + ny * ny + nz * nz)
    along = {1: nx, 3: ny, 5: nz, 7: nx + ny, 9: nx - ny, 11: nx + nz, 13: nx - nz, 15: ny + nz, 17: ny - nz}
    keep = 1.0 - omega_rate
    post = {0: base + keep * g[0]}
    for i, t in along.items():
        even = base + k * (t * t)
        post[i] = (even + t) + keep * g[i]
        post[i + 1] = (even - t) + keep * g[i + 1]
    return post


def kernel(n, rows, pops, heights, out, held, stage, walls, in_sem, out_sem, sent_up, sent_down, got_up, got_down, wall_sem):
    width, depth, lanes = pops.shape[1], pops.shape[2], pops.shape[3]
    chunks = depth // rows
    me = lax.axis_index("gx")
    right, left = lax.rem(me + 1, n), lax.rem(me + n - 1, n)
    edges = [1, width] if width > 1 else [1]
    inner = list(range(2, width))

    fetches = {}
    for plane in edges + inner:
        fetches[plane] = pltpu.make_async_copy(pops.at[:, plane - 1], stage.at[:, plane - 1], in_sem.at[plane - 1])
        fetches[plane].start()

    barrier = pltpu.get_barrier_semaphore()
    for neighbour in (left, right):
        pl.semaphore_signal(barrier, inc=1, device_id={"gx": neighbour}, device_id_type=MESH)

    for plane in range(1, width + 1):
        walls[1, plane] = jnp.broadcast_to(heights[plane - 1 : plane, :], (rows, lanes))
    pl.semaphore_wait(barrier, 2)
    wall_up = pltpu.make_async_remote_copy(
        walls.at[1, width], walls.at[1, 0], wall_sem.at[0], wall_sem.at[1], device_id={"gx": right}, device_id_type=MESH)
    wall_down = pltpu.make_async_remote_copy(
        walls.at[1, 1], walls.at[1, width + 1], wall_sem.at[2], wall_sem.at[3], device_id={"gx": left}, device_id_type=MESH)
    wall_up.start()
    wall_down.start()

    def copies(step, chunk):
        slot = lax.rem(step, 2)
        span = pl.ds(pl.multiple_of(PAD + chunk * rows, 8), rows)
        up = pltpu.make_async_remote_copy(
            held.at[slot, pl.ds(0, MOVING), width, span], held.at[slot, pl.ds(0, MOVING), 0, span],
            sent_up.at[step, chunk], got_up.at[step, chunk], device_id={"gx": right}, device_id_type=MESH)
        down = pltpu.make_async_remote_copy(
            held.at[slot, pl.ds(MOVING, MOVING), 1, span], held.at[slot, pl.ds(MOVING, MOVING), width + 1, span],
            sent_down.at[step, chunk], got_down.at[step, chunk], device_id={"gx": left}, device_id_type=MESH)
        return up, down

    def arrived(step, chunk):
        for copy in copies(step, chunk):
            copy.wait_recv()

    def left_here(step, chunk):
        for copy in copies(step, chunk):
            copy.wait_send()

    def keep_post(slot, plane, first, post):
        span = pl.ds(pl.multiple_of(PAD + first, 8), rows)
        for i in range(19):
            held[slot, spot[i], plane, span, :] = post[i]

    def stream(slot, plane, first):
        z = lax.broadcasted_iota(jnp.int32, (rows, lanes), 0) + first
        source_z = {0: z, 1: z - 1, -1: jnp.where(z == depth - 1, -1, z + 1)}
        here = pl.ds(pl.multiple_of(PAD + first, 8), rows)
        post = {i: held[slot, spot[i], plane, here, :] for i in range(19)}
        g = {}
        for i in range(19):
            cx, cy, cz = velocity_table[i]
            if cx == 0 and cz == 0:
                moved = post[i]
            elif cz == 0:
                moved = held[slot, spot[i], plane - cx, here, :]
            else:
                moved = held[slot, spot[i], plane - cx, pl.ds(PAD + first - cz, rows), :]
            if cy != 0:
                moved = pltpu.roll(moved, cy % lanes, 1)
            fluid = source_z[cz] >= walls[1 + cy, plane - cx]
            g[i] = jnp.where(fluid, moved, post[opposite(i)])
        return g

    for plane in edges:
        fetches[plane].wait()

    def first_chunk(chunk, carry):
        first = chunk * rows
        span = pl.ds(pl.multiple_of(first, 8), rows)
        for plane in edges:
            keep_post(0, plane, first, collide({i: stage[i, plane - 1, span, :] for i in range(19)}))
        for copy in copies(0, chunk):
            copy.start()
        return carry

    lax.fori_loop(0, chunks, first_chunk, 0)
    for plane in inner:
        fetches[plane].wait()

    def first_inner(chunk, carry):
        first = chunk * rows
        span = pl.ds(pl.multiple_of(first, 8), rows)
        for plane in inner:
            keep_post(0, plane, first, collide({i: stage[i, plane - 1, span, :] for i in range(19)}))
        return carry

    lax.fori_loop(0, chunks, first_inner, 0)

    wall_up.wait()
    wall_down.wait()
    for plane in range(width + 2):
        for cy in (1, -1):
            walls[1 + cy, plane] = pltpu.roll(walls[1, plane], cy % lanes, 1)

    def one_step(step, carry):
        slot, before = lax.rem(step, 2), lax.rem(step + 1, 2)
        arrived(step - 1, 0)

        def one_chunk(chunk, inside):
            first = chunk * rows

            @pl.when(chunk < chunks - 1)
            def _():
                arrived(step - 1, chunk + 1)

            @pl.when(step >= 2)
            def _():
                left_here(step - 2, chunk)

            for plane in edges:
                keep_post(slot, plane, first, collide(stream(before, plane, first)))
            for copy in copies(step, chunk):
                copy.start()
            for plane in inner:
                keep_post(slot, plane, first, collide(stream(before, plane, first)))
            return inside

        lax.fori_loop(0, chunks, one_chunk, 0)
        return carry

    lax.fori_loop(1, STEPS, one_step, 0)

    last = (STEPS - 1) % 2

    def write_back(chunk):
        span = pl.ds(pl.multiple_of(chunk * rows, 8), rows)
        return pltpu.make_async_copy(stage.at[:, :, span], out.at[:, :, span], out_sem.at[chunk])

    arrived(STEPS - 1, 0)

    def last_chunk(chunk, carry):
        first = chunk * rows
        span = pl.ds(pl.multiple_of(first, 8), rows)

        @pl.when(chunk < chunks - 1)
        def _():
            arrived(STEPS - 1, chunk + 1)

        for plane in range(1, width + 1):
            g = stream(last, plane, first)
            for i in range(19):
                stage[i, plane - 1, span, :] = g[i]
        write_back(chunk).start()
        return carry

    lax.fori_loop(0, chunks, last_chunk, 0)

    def finish(chunk, carry):
        left_here(STEPS - 2, chunk)
        left_here(STEPS - 1, chunk)
        write_back(chunk).wait()
        return carry

    lax.fori_loop(0, chunks, finish, 0)


def solution(mesh):
    n = mesh.shape["gx"]

    def per_device(pops, heights):
        kinds, width, depth, lanes = pops.shape
        rows = 16 if depth % 16 == 0 else 8
        chunks = depth // rows
        dma = pltpu.SemaphoreType.DMA
        return pl.pallas_call(
            functools.partial(kernel, n, rows),
            out_shape=jax.ShapeDtypeStruct(pops.shape, pops.dtype),
            in_specs=[pl.BlockSpec(memory_space=pl.ANY), pl.BlockSpec(memory_space=pltpu.VMEM)],
            out_specs=pl.BlockSpec(memory_space=pl.ANY),
            scratch_shapes=[
                pltpu.VMEM((2, kinds, width + 2, depth + 2 * PAD, lanes), jnp.float32),
                pltpu.VMEM(pops.shape, jnp.float32),
                pltpu.VMEM((3, width + 2, rows, lanes), jnp.int32),
                dma((width,)),
                dma((chunks,)),
                dma((STEPS, chunks)),
                dma((STEPS, chunks)),
                dma((STEPS, chunks)),
                dma((STEPS, chunks)),
                dma((4,)),
            ],
            compiler_params=pltpu.CompilerParams(
                collective_id=0, has_side_effects=True, vmem_limit_bytes=32 * 1024 * 1024
            ),
            cost_estimate=pl.CostEstimate(
                flops=250 * STEPS * width * depth * lanes, bytes_accessed=8 * pops.size, transcendentals=0
            ),
        )(pops, heights)

    return jax.shard_map(
        per_device,
        mesh=mesh,
        in_specs=(P(None, ("dir", "gx"), None, None), P(("dir", "gx"), None)),
        out_specs=P(None, ("dir", "gx"), None, None),
        check_vma=False,
    )
```

```python
import functools

import jax
import jax.numpy as jnp
from jax import lax
from jax.experimental import pallas as pl
from jax.experimental.pallas import tpu as pltpu
from jax.sharding import PartitionSpec as P

STEPS = 6
PAD = 8
MESH = pl.DeviceIdType.MESH

velocity_table = [
    (0, 0, 0),
    (1, 0, 0),
    (-1, 0, 0),
    (0, 1, 0),
    (0, -1, 0),
    (0, 0, 1),
    (0, 0, -1),
    (1, 1, 0),
    (-1, -1, 0),
    (1, -1, 0),
    (-1, 1, 0),
    (1, 0, 1),
    (-1, 0, -1),
    (1, 0, -1),
    (-1, 0, 1),
    (0, 1, 1),
    (0, -1, -1),
    (0, 1, -1),
    (0, -1, 1),
]
omega_rate = 1.9
held_order = [1, 7, 9, 11, 13, 2, 8, 10, 12, 14, 0, 3, 4, 5, 6, 15, 16, 17, 18]
spot = {component: place for place, component in enumerate(held_order)}
MOVING = 5


def opposite(component):
    if component == 0:
        return 0
    return component + 1 if component % 2 == 1 else component - 1


def collide(g):
    sums = {i: g[i] + g[i + 1] for i in range(1, 19, 2)}
    diffs = {i: g[i] - g[i + 1] for i in range(1, 19, 2)}
    axis_sum = sums[1] + sums[3] + sums[5]
    cross_sum = (sums[7] + sums[9]) + (sums[11] + sums[13]) + (sums[15] + sums[17])
    total = 12.0 * g[0] + 2.0 * axis_sum + cross_sum
    scale = 3.0 * omega_rate / 36.0
    nx = scale * (2.0 * diffs[1] + ((diffs[7] + diffs[9]) + (diffs[11] + diffs[13])))
    ny = scale * (2.0 * diffs[3] + ((diffs[7] - diffs[9]) + (diffs[15] + diffs[17])))
    nz = scale * (2.0 * diffs[5] + ((diffs[11] - diffs[13]) + (diffs[15] - diffs[17])))
    k = (omega_rate * 4.5 / 36.0 / (scale * scale)) / total
    base = (omega_rate / 36.0) * total - (k * (1.0 / 3.0)) * (nx * nx + ny * ny + nz * nz)
    along = {1: nx, 3: ny, 5: nz, 7: nx + ny, 9: nx - ny, 11: nx + nz, 13: nx - nz, 15: ny + nz, 17: ny - nz}
    keep = 1.0 - omega_rate
    post = {0: base + keep * g[0]}
    for i, t in along.items():
        even = base + k * (t * t)
        post[i] = (even + t) + keep * g[i]
        post[i + 1] = (even - t) + keep * g[i + 1]
    return post


def kernel(n, rows, pops, heights, out, held, stage, walls, ground, ground_sem, in_sem, out_sem, sent_up, sent_down, got_up, got_down, wall_sem):
    width, depth, lanes = pops.shape[1], pops.shape[2], pops.shape[3]
    chunks = depth // rows
    me = lax.axis_index("gx")
    right, left = lax.rem(me + 1, n), lax.rem(me + n - 1, n)
    edges = [1, width] if width > 1 else [1]
    inner = list(range(2, width))

    ground_fetch = pltpu.make_async_copy(heights, ground, ground_sem)
    ground_fetch.start()
    fetches = {}
    for plane in edges + inner:
        fetches[plane] = pltpu.make_async_copy(pops.at[:, plane - 1], stage.at[:, plane - 1], in_sem.at[plane - 1])
        fetches[plane].start()

    barrier = pltpu.get_barrier_semaphore()
    for neighbour in (left, right):
        pl.semaphore_signal(barrier, inc=1, device_id={"gx": neighbour}, device_id_type=MESH)

    wall_up = pltpu.make_async_remote_copy(
        walls.at[1, width], walls.at[1, 0], wall_sem.at[0], wall_sem.at[1], device_id={"gx": right}, device_id_type=MESH)
    wall_down = pltpu.make_async_remote_copy(
        walls.at[1, 1], walls.at[1, width + 1], wall_sem.at[2], wall_sem.at[3], device_id={"gx": left}, device_id_type=MESH)

    def copies(step, chunk):
        slot = lax.rem(step, 2)
        span = pl.ds(pl.multiple_of(PAD + chunk * rows, 8), rows)
        up = pltpu.make_async_remote_copy(
            held.at[slot, pl.ds(0, MOVING), width, span], held.at[slot, pl.ds(0, MOVING), 0, span],
            sent_up.at[step, chunk], got_up.at[step, chunk], device_id={"gx": right}, device_id_type=MESH)
        down = pltpu.make_async_remote_copy(
            held.at[slot, pl.ds(MOVING, MOVING), 1, span], held.at[slot, pl.ds(MOVING, MOVING), width + 1, span],
            sent_down.at[step, chunk], got_down.at[step, chunk], device_id={"gx": left}, device_id_type=MESH)
        return up, down

    def arrived(step, chunk):
        for copy in copies(step, chunk):
            copy.wait_recv()

    def left_here(step, chunk):
        for copy in copies(step, chunk):
            copy.wait_send()

    def keep_post(slot, plane, first, post):
        span = pl.ds(pl.multiple_of(PAD + first, 8), rows)
        for i in range(19):
            held[slot, spot[i], plane, span, :] = post[i]

    def stream(slot, plane, first):
        z = lax.broadcasted_iota(jnp.int32, (rows, lanes), 0) + first
        source_z = {0: z, 1: z - 1, -1: jnp.where(z == depth - 1, -1, z + 1)}
        here = pl.ds(pl.multiple_of(PAD + first, 8), rows)
        post = {i: held[slot, spot[i], plane, here, :] for i in range(19)}
        g = {}
        for i in range(19):
            cx, cy, cz = velocity_table[i]
            if cx == 0 and cz == 0:
                moved = post[i]
            elif cz == 0:
                moved = held[slot, spot[i], plane - cx, here, :]
            else:
                moved = held[slot, spot[i], plane - cx, pl.ds(PAD + first - cz, rows), :]
            if cy != 0:
                moved = pltpu.roll(moved, cy % lanes, 1)
            fluid = source_z[cz] >= walls[1 + cy, plane - cx]
            g[i] = jnp.where(fluid, moved, post[opposite(i)])
        return g

    def first_post(planes, chunk):
        first = chunk * rows
        span = pl.ds(pl.multiple_of(first, 8), rows)
        for plane in planes:
            keep_post(0, plane, first, collide({i: stage[i, plane - 1, span, :] for i in range(19)}))

    ground_fetch.wait()
    for plane in range(1, width + 1):
        walls[1, plane] = jnp.broadcast_to(ground[plane - 1 : plane, :], (rows, lanes))
    for plane in edges:
        fetches[plane].wait()
    first_post(edges, 0)
    pl.semaphore_wait(barrier, 2)
    wall_up.start()
    wall_down.start()
    for copy in copies(0, 0):
        copy.start()

    def first_chunk(chunk, carry):
        first_post(edges, chunk)
        for copy in copies(0, chunk):
            copy.start()
        return carry

    lax.fori_loop(1, chunks, first_chunk, 0)
    for plane in inner:
        fetches[plane].wait()

    def first_inner(chunk, carry):
        first_post(inner, chunk)
        return carry

    lax.fori_loop(0, chunks, first_inner, 0)

    wall_up.wait()
    wall_down.wait()
    for plane in range(width + 2):
        for cy in (1, -1):
            walls[1 + cy, plane] = pltpu.roll(walls[1, plane], cy % lanes, 1)

    def one_step(step, carry):
        slot, before = lax.rem(step, 2), lax.rem(step + 1, 2)
        arrived(step - 1, 0)

        def one_chunk(chunk, inside):
            first = chunk * rows

            @pl.when(chunk < chunks - 1)
            def _():
                arrived(step - 1, chunk + 1)

            @pl.when(step >= 2)
            def _():
                left_here(step - 2, chunk)

            for plane in edges:
                keep_post(slot, plane, first, collide(stream(before, plane, first)))
            for copy in copies(step, chunk):
                copy.start()
            for plane in inner:
                keep_post(slot, plane, first, collide(stream(before, plane, first)))
            return inside

        lax.fori_loop(0, chunks, one_chunk, 0)
        return carry

    lax.fori_loop(1, STEPS, one_step, 0)

    last = (STEPS - 1) % 2

    def write_back(chunk):
        span = pl.ds(pl.multiple_of(chunk * rows, 8), rows)
        return pltpu.make_async_copy(stage.at[:, :, span], out.at[:, :, span], out_sem.at[chunk])

    arrived(STEPS - 1, 0)

    def last_chunk(chunk, carry):
        first = chunk * rows
        span = pl.ds(pl.multiple_of(first, 8), rows)

        @pl.when(chunk < chunks - 1)
        def _():
            arrived(STEPS - 1, chunk + 1)

        for plane in range(1, width + 1):
            g = stream(last, plane, first)
            for i in range(19):
                stage[i, plane - 1, span, :] = g[i]
        write_back(chunk).start()
        return carry

    lax.fori_loop(0, chunks, last_chunk, 0)

    def finish(chunk, carry):
        left_here(STEPS - 2, chunk)
        left_here(STEPS - 1, chunk)
        write_back(chunk).wait()
        return carry

    lax.fori_loop(0, chunks, finish, 0)


def solution(mesh):
    n = mesh.shape["gx"]

    def per_device(pops, heights):
        kinds, width, depth, lanes = pops.shape
        rows = 8
        chunks = depth // rows
        dma = pltpu.SemaphoreType.DMA
        return pl.pallas_call(
            functools.partial(kernel, n, rows),
            out_shape=jax.ShapeDtypeStruct(pops.shape, pops.dtype),
            in_specs=[pl.BlockSpec(memory_space=pltpu.HBM)] * 2,
            out_specs=pl.BlockSpec(memory_space=pltpu.HBM),
            scratch_shapes=[
                pltpu.VMEM((2, kinds, width + 2, depth + 2 * PAD, lanes), jnp.float32),
                pltpu.VMEM(pops.shape, jnp.float32),
                pltpu.VMEM((3, width + 2, rows, lanes), jnp.int32),
                pltpu.VMEM(heights.shape, jnp.int32),
                dma,
                dma((width,)),
                dma((chunks,)),
                dma((STEPS, chunks)),
                dma((STEPS, chunks)),
                dma((STEPS, chunks)),
                dma((STEPS, chunks)),
                dma((4,)),
            ],
            compiler_params=pltpu.CompilerParams(
                collective_id=0, has_side_effects=True, vmem_limit_bytes=32 * 1024 * 1024
            ),
            cost_estimate=pl.CostEstimate(
                flops=250 * STEPS * width * depth * lanes, bytes_accessed=8 * pops.size, transcendentals=0
            ),
        )(pops, heights)

    return jax.shard_map(
        per_device,
        mesh=mesh,
        in_specs=(P(None, ("dir", "gx"), None, None), P(("dir", "gx"), None)),
        out_specs=P(None, ("dir", "gx"), None, None),
        check_vma=False,
    )
```

```python
import functools

import jax
import jax.numpy as jnp
from jax import lax
from jax.experimental import pallas as pl
from jax.experimental.pallas import tpu as pltpu
from jax.sharding import PartitionSpec as P

STEPS = 6
PAD = 8
MESH = pl.DeviceIdType.MESH

velocity_table = [
    (0, 0, 0),
    (1, 0, 0),
    (-1, 0, 0),
    (0, 1, 0),
    (0, -1, 0),
    (0, 0, 1),
    (0, 0, -1),
    (1, 1, 0),
    (-1, -1, 0),
    (1, -1, 0),
    (-1, 1, 0),
    (1, 0, 1),
    (-1, 0, -1),
    (1, 0, -1),
    (-1, 0, 1),
    (0, 1, 1),
    (0, -1, -1),
    (0, 1, -1),
    (0, -1, 1),
]
omega_rate = 1.9
held_order = [1, 7, 9, 11, 13, 2, 8, 10, 12, 14, 0, 3, 4, 5, 6, 15, 16, 17, 18]
spot = {component: place for place, component in enumerate(held_order)}
MOVING = 5


def opposite(component):
    if component == 0:
        return 0
    return component + 1 if component % 2 == 1 else component - 1


def collide(g):
    sums = {i: g[i] + g[i + 1] for i in range(1, 19, 2)}
    diffs = {i: g[i] - g[i + 1] for i in range(1, 19, 2)}
    axis_sum = sums[1] + sums[3] + sums[5]
    cross_sum = (sums[7] + sums[9]) + (sums[11] + sums[13]) + (sums[15] + sums[17])
    total = 12.0 * g[0] + 2.0 * axis_sum + cross_sum
    scale = 3.0 * omega_rate / 36.0
    nx = scale * (2.0 * diffs[1] + ((diffs[7] + diffs[9]) + (diffs[11] + diffs[13])))
    ny = scale * (2.0 * diffs[3] + ((diffs[7] - diffs[9]) + (diffs[15] + diffs[17])))
    nz = scale * (2.0 * diffs[5] + ((diffs[11] - diffs[13]) + (diffs[15] - diffs[17])))
    k = (omega_rate * 4.5 / 36.0 / (scale * scale)) / total
    base = (omega_rate / 36.0) * total - (k * (1.0 / 3.0)) * (nx * nx + ny * ny + nz * nz)
    along = {1: nx, 3: ny, 5: nz, 7: nx + ny, 9: nx - ny, 11: nx + nz, 13: nx - nz, 15: ny + nz, 17: ny - nz}
    keep = 1.0 - omega_rate
    post = {0: base + keep * g[0]}
    for i, t in along.items():
        even = base + k * (t * t)
        post[i] = (even + t) + keep * g[i]
        post[i + 1] = (even - t) + keep * g[i + 1]
    return post


def kernel(n, rows, pops, heights, out, even_post, odd_post, stage, walls, ground, ground_sem, in_sem, out_sem, sent_up, sent_down, got_up, got_down, wall_sem):
    width, depth, lanes = pops.shape[1], pops.shape[2], pops.shape[3]
    chunks = depth // rows
    me = lax.axis_index("gx")
    right, left = lax.rem(me + 1, n), lax.rem(me + n - 1, n)
    edges = [1, width] if width > 1 else [1]
    inner = list(range(2, width))

    ground_fetch = pltpu.make_async_copy(heights, ground, ground_sem)
    ground_fetch.start()
    fetches = {}
    for plane in edges + inner:
        fetches[plane] = pltpu.make_async_copy(pops.at[:, plane - 1], stage.at[:, plane - 1], in_sem.at[plane - 1])
        fetches[plane].start()

    barrier = pltpu.get_barrier_semaphore()
    for neighbour in (left, right):
        pl.semaphore_signal(barrier, inc=1, device_id={"gx": neighbour}, device_id_type=MESH)

    wall_up = pltpu.make_async_remote_copy(
        walls.at[1, width], walls.at[1, 0], wall_sem.at[0], wall_sem.at[1], device_id={"gx": right}, device_id_type=MESH)
    wall_down = pltpu.make_async_remote_copy(
        walls.at[1, 1], walls.at[1, width + 1], wall_sem.at[2], wall_sem.at[3], device_id={"gx": left}, device_id_type=MESH)

    def copies(held, step, chunk):
        span = pl.ds(pl.multiple_of(PAD + chunk * rows, 8), rows)
        up = pltpu.make_async_remote_copy(
            held.at[pl.ds(0, MOVING), width, span], held.at[pl.ds(0, MOVING), 0, span],
            sent_up.at[step, chunk], got_up.at[step, chunk], device_id={"gx": right}, device_id_type=MESH)
        down = pltpu.make_async_remote_copy(
            held.at[pl.ds(MOVING, MOVING), 1, span], held.at[pl.ds(MOVING, MOVING), width + 1, span],
            sent_down.at[step, chunk], got_down.at[step, chunk], device_id={"gx": left}, device_id_type=MESH)
        return up, down

    def arrived(held, step, chunk):
        for copy in copies(held, step, chunk):
            copy.wait_recv()

    def left_here(held, step, chunk):
        for copy in copies(held, step, chunk):
            copy.wait_send()

    def keep_post(held, first, posts):
        span = pl.ds(pl.multiple_of(PAD + first, 8), rows)
        for plane, post in posts.items():
            for i in range(19):
                held[spot[i], plane, span, :] = post[i]

    def stream(held, plane, first):
        z = lax.broadcasted_iota(jnp.int32, (rows, lanes), 0) + first
        source_z = {0: z, 1: z - 1, -1: jnp.where(z == depth - 1, -1, z + 1)}
        here = pl.ds(pl.multiple_of(PAD + first, 8), rows)
        post = {i: held[spot[i], plane, here, :] for i in range(19)}
        g = {}
        for i in range(19):
            cx, cy, cz = velocity_table[i]
            if cx == 0 and cz == 0:
                moved = post[i]
            elif cz == 0:
                moved = held[spot[i], plane - cx, here, :]
            else:
                moved = held[spot[i], plane - cx, pl.ds(PAD + first - cz, rows), :]
            if cy != 0:
                moved = pltpu.roll(moved, cy % lanes, 1)
            fluid = source_z[cz] >= walls[1 + cy, plane - cx]
            g[i] = jnp.where(fluid, moved, post[opposite(i)])
        return g

    def first_post(planes, chunk):
        first = chunk * rows
        span = pl.ds(pl.multiple_of(first, 8), rows)
        keep_post(even_post, first, {
            plane: collide({i: stage[i, plane - 1, span, :] for i in range(19)}) for plane in planes
        })

    ground_fetch.wait()
    for plane in range(1, width + 1):
        walls[1, plane] = jnp.broadcast_to(ground[plane - 1 : plane, :], (rows, lanes))
    for plane in edges:
        fetches[plane].wait()
    first_post(edges, 0)
    pl.semaphore_wait(barrier, 2)
    wall_up.start()
    wall_down.start()
    for copy in copies(even_post, 0, 0):
        copy.start()

    def first_chunk(chunk, carry):
        first_post(edges, chunk)
        for copy in copies(even_post, 0, chunk):
            copy.start()
        return carry

    lax.fori_loop(1, chunks, first_chunk, 0)
    for plane in inner:
        fetches[plane].wait()

    def first_inner(chunk, carry):
        first_post(inner, chunk)
        return carry

    lax.fori_loop(0, chunks, first_inner, 0)

    wall_up.wait()
    wall_down.wait()
    for plane in range(width + 2):
        for cy in (1, -1):
            walls[1 + cy, plane] = pltpu.roll(walls[1, plane], cy % lanes, 1)

    def one_step(step, before, held):
        arrived(before, step - 1, 0)

        def one_chunk(chunk, inside):
            first = chunk * rows

            @pl.when(chunk < chunks - 1)
            def _():
                arrived(before, step - 1, chunk + 1)

            @pl.when(step >= 2)
            def _():
                left_here(held, step - 2, chunk)

            keep_post(held, first, {plane: collide(stream(before, plane, first)) for plane in edges})
            for copy in copies(held, step, chunk):
                copy.start()
            keep_post(held, first, {plane: collide(stream(before, plane, first)) for plane in inner})
            return inside

        lax.fori_loop(0, chunks, one_chunk, 0)

    def two_steps(pair, carry):
        one_step(2 * pair + 1, even_post, odd_post)
        one_step(2 * pair + 2, odd_post, even_post)
        return carry

    lax.fori_loop(0, (STEPS - 1) // 2, two_steps, 0)
    if STEPS % 2 == 0:
        one_step(STEPS - 1, even_post, odd_post)
    last, other = (odd_post, even_post) if STEPS % 2 == 0 else (even_post, odd_post)

    def write_back(chunk):
        span = pl.ds(pl.multiple_of(chunk * rows, 8), rows)
        return pltpu.make_async_copy(stage.at[:, :, span], out.at[:, :, span], out_sem.at[chunk])

    arrived(last, STEPS - 1, 0)

    def last_chunk(chunk, carry):
        first = chunk * rows
        span = pl.ds(pl.multiple_of(first, 8), rows)

        @pl.when(chunk < chunks - 1)
        def _():
            arrived(last, STEPS - 1, chunk + 1)

        for plane in range(1, width + 1):
            g = stream(last, plane, first)
            for i in range(19):
                stage[i, plane - 1, span, :] = g[i]
        write_back(chunk).start()
        return carry

    lax.fori_loop(0, chunks, last_chunk, 0)

    def finish(chunk, carry):
        left_here(other, STEPS - 2, chunk)
        left_here(last, STEPS - 1, chunk)
        write_back(chunk).wait()
        return carry

    lax.fori_loop(0, chunks, finish, 0)


def solution(mesh):
    n = mesh.shape["gx"]

    def per_device(pops, heights):
        kinds, width, depth, lanes = pops.shape
        rows = 8
        chunks = depth // rows
        dma = pltpu.SemaphoreType.DMA
        return pl.pallas_call(
            functools.partial(kernel, n, rows),
            out_shape=jax.ShapeDtypeStruct(pops.shape, pops.dtype),
            in_specs=[pl.BlockSpec(memory_space=pltpu.HBM)] * 2,
            out_specs=pl.BlockSpec(memory_space=pltpu.HBM),
            scratch_shapes=[
                pltpu.VMEM((kinds, width + 2, depth + 2 * PAD, lanes), jnp.float32),
                pltpu.VMEM((kinds, width + 2, depth + 2 * PAD, lanes), jnp.float32),
                pltpu.VMEM(pops.shape, jnp.float32),
                pltpu.VMEM((3, width + 2, rows, lanes), jnp.int32),
                pltpu.VMEM(heights.shape, jnp.int32),
                dma,
                dma((width,)),
                dma((chunks,)),
                dma((STEPS, chunks)),
                dma((STEPS, chunks)),
                dma((STEPS, chunks)),
                dma((STEPS, chunks)),
                dma((4,)),
            ],
            compiler_params=pltpu.CompilerParams(
                collective_id=0, has_side_effects=True, vmem_limit_bytes=62 * 1024 * 1024
            ),
            cost_estimate=pl.CostEstimate(
                flops=250 * STEPS * width * depth * lanes, bytes_accessed=8 * pops.size, transcendentals=0
            ),
        )(pops, heights)

    return jax.shard_map(
        per_device,
        mesh=mesh,
        in_specs=(P(None, ("dir", "gx"), None, None), P(("dir", "gx"), None)),
        out_specs=P(None, ("dir", "gx"), None, None),
        check_vma=False,
    )
```

```python
import functools

import jax
import jax.numpy as jnp
from jax import lax
from jax.experimental import pallas as pl
from jax.experimental.pallas import tpu as pltpu
from jax.sharding import PartitionSpec as P

STEPS = 6
PAD = 8
MESH = pl.DeviceIdType.MESH

velocity_table = [
    (0, 0, 0),
    (1, 0, 0),
    (-1, 0, 0),
    (0, 1, 0),
    (0, -1, 0),
    (0, 0, 1),
    (0, 0, -1),
    (1, 1, 0),
    (-1, -1, 0),
    (1, -1, 0),
    (-1, 1, 0),
    (1, 0, 1),
    (-1, 0, -1),
    (1, 0, -1),
    (-1, 0, 1),
    (0, 1, 1),
    (0, -1, -1),
    (0, 1, -1),
    (0, -1, 1),
]
omega_rate = 1.9
held_order = [1, 7, 9, 11, 13, 2, 8, 10, 12, 14, 0, 3, 4, 5, 6, 15, 16, 17, 18]
spot = {component: place for place, component in enumerate(held_order)}
MOVING = 5


def opposite(component):
    if component == 0:
        return 0
    return component + 1 if component % 2 == 1 else component - 1


def collide(g):
    sums = {i: g[i] + g[i + 1] for i in range(1, 19, 2)}
    diffs = {i: g[i] - g[i + 1] for i in range(1, 19, 2)}
    axis_sum = sums[1] + sums[3] + sums[5]
    cross_sum = (sums[7] + sums[9]) + (sums[11] + sums[13]) + (sums[15] + sums[17])
    total = 12.0 * g[0] + 2.0 * axis_sum + cross_sum
    scale = 3.0 * omega_rate / 36.0
    nx = scale * (2.0 * diffs[1] + ((diffs[7] + diffs[9]) + (diffs[11] + diffs[13])))
    ny = scale * (2.0 * diffs[3] + ((diffs[7] - diffs[9]) + (diffs[15] + diffs[17])))
    nz = scale * (2.0 * diffs[5] + ((diffs[11] - diffs[13]) + (diffs[15] - diffs[17])))
    k = (omega_rate * 4.5 / 36.0 / (scale * scale)) / total
    base = (omega_rate / 36.0) * total - (k * (1.0 / 3.0)) * (nx * nx + ny * ny + nz * nz)
    along = {1: nx, 3: ny, 5: nz, 7: nx + ny, 9: nx - ny, 11: nx + nz, 13: nx - nz, 15: ny + nz, 17: ny - nz}
    keep = 1.0 - omega_rate
    post = {0: base + keep * g[0]}
    for i, t in along.items():
        even = base + k * (t * t)
        post[i] = (even + t) + keep * g[i]
        post[i + 1] = (even - t) + keep * g[i + 1]
    return post


def stream(walls, rows, depth, held, plane, first):
    lanes = held.shape[-1]
    z = lax.broadcasted_iota(jnp.int32, (rows, lanes), 0) + first
    source_z = {0: z, 1: z - 1, -1: jnp.where(z == depth - 1, -1, z + 1)}
    here = pl.ds(pl.multiple_of(PAD + first, 8), rows)
    post = {i: held[spot[i], plane, here, :] for i in range(19)}
    g = {}
    for i in range(19):
        cx, cy, cz = velocity_table[i]
        if cx == 0 and cz == 0:
            moved = post[i]
        elif cz == 0:
            moved = held[spot[i], plane - cx, here, :]
        else:
            moved = held[spot[i], plane - cx, pl.ds(PAD + first - cz, rows), :]
        if cy != 0:
            moved = pltpu.roll(moved, cy % lanes, 1)
        fluid = source_z[cz] >= walls[1 + cy, plane - cx]
        g[i] = jnp.where(fluid, moved, post[opposite(i)])
    return g


def kernel(n, rows, pops, heights, last_post, walls, stage, other_post, ground, ground_sem, in_sem, sent_up, sent_down, got_up, got_down, wall_sem):
    width, depth, lanes = pops.shape[1], pops.shape[2], pops.shape[3]
    chunks = depth // rows
    even_post, odd_post = (other_post, last_post) if STEPS % 2 == 0 else (last_post, other_post)
    me = lax.axis_index("gx")
    right, left = lax.rem(me + 1, n), lax.rem(me + n - 1, n)
    edges = [1, width] if width > 1 else [1]
    inner = list(range(2, width))

    ground_fetch = pltpu.make_async_copy(heights, ground, ground_sem)
    ground_fetch.start()
    fetches = {}
    for plane in edges + inner:
        fetches[plane] = pltpu.make_async_copy(pops.at[:, plane - 1], stage.at[:, plane - 1], in_sem.at[plane - 1])
        fetches[plane].start()

    barrier = pltpu.get_barrier_semaphore()
    for neighbour in (left, right):
        pl.semaphore_signal(barrier, inc=1, device_id={"gx": neighbour}, device_id_type=MESH)

    wall_up = pltpu.make_async_remote_copy(
        walls.at[1, width], walls.at[1, 0], wall_sem.at[0], wall_sem.at[1], device_id={"gx": right}, device_id_type=MESH)
    wall_down = pltpu.make_async_remote_copy(
        walls.at[1, 1], walls.at[1, width + 1], wall_sem.at[2], wall_sem.at[3], device_id={"gx": left}, device_id_type=MESH)

    def copies(held, step, chunk):
        span = pl.ds(pl.multiple_of(PAD + chunk * rows, 8), rows)
        up = pltpu.make_async_remote_copy(
            held.at[pl.ds(0, MOVING), width, span], held.at[pl.ds(0, MOVING), 0, span],
            sent_up.at[step, chunk], got_up.at[step, chunk], device_id={"gx": right}, device_id_type=MESH)
        down = pltpu.make_async_remote_copy(
            held.at[pl.ds(MOVING, MOVING), 1, span], held.at[pl.ds(MOVING, MOVING), width + 1, span],
            sent_down.at[step, chunk], got_down.at[step, chunk], device_id={"gx": left}, device_id_type=MESH)
        return up, down

    def arrived(held, step, chunk):
        for copy in copies(held, step, chunk):
            copy.wait_recv()

    def left_here(held, step, chunk):
        for copy in copies(held, step, chunk):
            copy.wait_send()

    def keep_post(held, first, posts):
        span = pl.ds(pl.multiple_of(PAD + first, 8), rows)
        for plane, post in posts.items():
            for i in range(19):
                held[spot[i], plane, span, :] = post[i]

    stream_here = functools.partial(stream, walls, rows, depth)

    def first_post(planes, chunk):
        first = chunk * rows
        span = pl.ds(pl.multiple_of(first, 8), rows)
        keep_post(even_post, first, {
            plane: collide({i: stage[i, plane - 1, span, :] for i in range(19)}) for plane in planes
        })

    ground_fetch.wait()
    for plane in range(1, width + 1):
        walls[1, plane] = jnp.broadcast_to(ground[plane - 1 : plane, :], (rows, lanes))
    for plane in edges:
        fetches[plane].wait()
    first_post(edges, 0)
    pl.semaphore_wait(barrier, 2)
    wall_up.start()
    wall_down.start()
    for copy in copies(even_post, 0, 0):
        copy.start()

    def first_chunk(chunk, carry):
        first_post(edges, chunk)
        for copy in copies(even_post, 0, chunk):
            copy.start()
        return carry

    lax.fori_loop(1, chunks, first_chunk, 0)
    for plane in inner:
        fetches[plane].wait()

    def first_inner(chunk, carry):
        first_post(inner, chunk)
        return carry

    lax.fori_loop(0, chunks, first_inner, 0)

    wall_up.wait()
    wall_down.wait()
    for plane in range(width + 2):
        for cy in (1, -1):
            walls[1 + cy, plane] = pltpu.roll(walls[1, plane], cy % lanes, 1)

    def one_step(step, before, held):
        arrived(before, step - 1, 0)

        def one_chunk(chunk, inside):
            first = chunk * rows

            @pl.when(chunk < chunks - 1)
            def _():
                arrived(before, step - 1, chunk + 1)

            @pl.when(step >= 2)
            def _():
                left_here(held, step - 2, chunk)

            keep_post(held, first, {plane: collide(stream_here(before, plane, first)) for plane in edges})
            for copy in copies(held, step, chunk):
                copy.start()
            keep_post(held, first, {plane: collide(stream_here(before, plane, first)) for plane in inner})
            return inside

        lax.fori_loop(0, chunks, one_chunk, 0)

    def two_steps(pair, carry):
        one_step(2 * pair + 1, even_post, odd_post)
        one_step(2 * pair + 2, odd_post, even_post)
        return carry

    lax.fori_loop(0, (STEPS - 1) // 2, two_steps, 0)
    if STEPS % 2 == 0:
        one_step(STEPS - 1, even_post, odd_post)

    def last_inner(chunk, carry):
        first = chunk * rows
        span = pl.ds(pl.multiple_of(first, 8), rows)
        streamed = {plane: stream_here(last_post, plane, first) for plane in inner}
        for plane, g in streamed.items():
            for i in range(19):
                stage[i, plane - 1, span, :] = g[i]
        return carry

    lax.fori_loop(0, chunks, last_inner, 0)

    def finish(chunk, carry):
        left_here(other_post, STEPS - 2, chunk)
        left_here(last_post, STEPS - 1, chunk)
        arrived(last_post, STEPS - 1, chunk)
        return carry

    lax.fori_loop(0, chunks, finish, 0)


def last_kernel(rows, last_post, walls, stage, out, ends, inner_sem, out_sem):
    width, depth = stage.shape[1], stage.shape[2]
    chunks = depth // rows
    edges = [1, width] if width > 1 else [1]
    inner_copies = [
        pltpu.make_async_copy(stage.at[:, plane - 1], out.at[:, plane - 1], inner_sem.at[plane - 1])
        for plane in range(2, width)
    ]
    for copy in inner_copies:
        copy.start()

    def write_back(chunk):
        span = pl.ds(pl.multiple_of(chunk * rows, 8), rows)
        return [
            pltpu.make_async_copy(ends.at[:, place, span], out.at[:, plane - 1, span], out_sem.at[chunk, place])
            for place, plane in enumerate(edges)
        ]

    def one_chunk(chunk, carry):
        first = chunk * rows
        span = pl.ds(pl.multiple_of(first, 8), rows)
        streamed = [stream(walls, rows, depth, last_post, plane, first) for plane in edges]
        for place, g in enumerate(streamed):
            for i in range(19):
                ends[i, place, span, :] = g[i]
        for copy in write_back(chunk):
            copy.start()
        return carry

    lax.fori_loop(0, chunks, one_chunk, 0)

    def finish(chunk, carry):
        for copy in write_back(chunk):
            copy.wait()
        return carry

    lax.fori_loop(0, chunks, finish, 0)
    for copy in inner_copies:
        copy.wait()


def solution(mesh):
    n = mesh.shape["gx"]

    def per_device(pops, heights):
        kinds, width, depth, lanes = pops.shape
        rows = 8
        chunks = depth // rows
        dma = pltpu.SemaphoreType.DMA
        held_shape = (kinds, width + 2, depth + 2 * PAD, lanes)
        wall_shape = (3, width + 2, rows, lanes)
        hbm, vmem = pl.BlockSpec(memory_space=pltpu.HBM), pl.BlockSpec(memory_space=pltpu.VMEM)
        kept = pl.pallas_call(
            functools.partial(kernel, n, rows),
            out_shape=[
                pltpu.VMEM(held_shape, jnp.float32),
                pltpu.VMEM(wall_shape, jnp.int32),
                pltpu.VMEM(pops.shape, jnp.float32),
            ],
            in_specs=[hbm] * 2,
            out_specs=[vmem] * 3,
            scratch_shapes=[
                pltpu.VMEM(held_shape, jnp.float32),
                pltpu.VMEM(heights.shape, jnp.int32),
                dma,
                dma((width,)),
                dma((STEPS, chunks)),
                dma((STEPS, chunks)),
                dma((STEPS, chunks)),
                dma((STEPS, chunks)),
                dma((4,)),
            ],
            compiler_params=pltpu.CompilerParams(
                collective_id=0, has_side_effects=True, vmem_limit_bytes=55 * 1024 * 1024
            ),
            cost_estimate=pl.CostEstimate(
                flops=250 * STEPS * width * depth * lanes, bytes_accessed=4 * pops.size, transcendentals=0
            ),
        )(pops, heights)
        return pl.pallas_call(
            functools.partial(last_kernel, rows),
            out_shape=jax.ShapeDtypeStruct(pops.shape, pops.dtype),
            in_specs=[vmem] * 3,
            out_specs=hbm,
            scratch_shapes=[
                pltpu.VMEM((kinds, min(width, 2), depth, lanes), jnp.float32),
                dma((width,)),
                dma((chunks, 2)),
            ],
            compiler_params=pltpu.CompilerParams(vmem_limit_bytes=32 * 1024 * 1024),
            cost_estimate=pl.CostEstimate(flops=20 * pops.size, bytes_accessed=4 * pops.size, transcendentals=0),
        )(*kept)

    return jax.shard_map(
        per_device,
        mesh=mesh,
        in_specs=(P(None, ("dir", "gx"), None, None), P(("dir", "gx"), None)),
        out_specs=P(None, ("dir", "gx"), None, None),
        check_vma=False,
    )
```

```python
import functools

import jax
import jax.numpy as jnp
from jax import lax
from jax.experimental import pallas as pl
from jax.experimental.pallas import tpu as pltpu
from jax.sharding import PartitionSpec as P

STEPS = 6
PAD = 8
MESH = pl.DeviceIdType.MESH

velocity_table = [
    (0, 0, 0),
    (1, 0, 0),
    (-1, 0, 0),
    (0, 1, 0),
    (0, -1, 0),
    (0, 0, 1),
    (0, 0, -1),
    (1, 1, 0),
    (-1, -1, 0),
    (1, -1, 0),
    (-1, 1, 0),
    (1, 0, 1),
    (-1, 0, -1),
    (1, 0, -1),
    (-1, 0, 1),
    (0, 1, 1),
    (0, -1, -1),
    (0, 1, -1),
    (0, -1, 1),
]
omega_rate = 1.9
held_order = [1, 7, 9, 11, 13, 2, 8, 10, 12, 14, 0, 3, 4, 5, 6, 15, 16, 17, 18]
spot = {component: place for place, component in enumerate(held_order)}
MOVING = 5


def opposite(component):
    if component == 0:
        return 0
    return component + 1 if component % 2 == 1 else component - 1


def collide(g):
    sums = {i: g[i] + g[i + 1] for i in range(1, 19, 2)}
    diffs = {i: g[i] - g[i + 1] for i in range(1, 19, 2)}
    axis_sum = sums[1] + sums[3] + sums[5]
    cross_sum = (sums[7] + sums[9]) + (sums[11] + sums[13]) + (sums[15] + sums[17])
    total = 12.0 * g[0] + 2.0 * axis_sum + cross_sum
    scale = 3.0 * omega_rate / 36.0
    nx = scale * (2.0 * diffs[1] + ((diffs[7] + diffs[9]) + (diffs[11] + diffs[13])))
    ny = scale * (2.0 * diffs[3] + ((diffs[7] - diffs[9]) + (diffs[15] + diffs[17])))
    nz = scale * (2.0 * diffs[5] + ((diffs[11] - diffs[13]) + (diffs[15] - diffs[17])))
    k = (omega_rate * 4.5 / 36.0 / (scale * scale)) / total
    base = (omega_rate / 36.0) * total - (k * (1.0 / 3.0)) * (nx * nx + ny * ny + nz * nz)
    along = {1: nx, 3: ny, 5: nz, 7: nx + ny, 9: nx - ny, 11: nx + nz, 13: nx - nz, 15: ny + nz, 17: ny - nz}
    keep = 1.0 - omega_rate
    post = {0: base + keep * g[0]}
    for i, t in along.items():
        even = base + k * (t * t)
        post[i] = (even + t) + keep * g[i]
        post[i + 1] = (even - t) + keep * g[i + 1]
    return post


def stream(walls, rows, depth, held, plane, first):
    lanes = held.shape[-1]
    z = lax.broadcasted_iota(jnp.int32, (rows, lanes), 0) + first
    source_z = {0: z, 1: z - 1, -1: jnp.where(z == depth - 1, -1, z + 1)}
    here = pl.ds(pl.multiple_of(PAD + first, 8), rows)
    post = {i: held[spot[i], plane, here, :] for i in range(19)}
    g = {}
    for i in range(19):
        cx, cy, cz = velocity_table[i]
        if cx == 0 and cz == 0:
            moved = post[i]
        elif cz == 0:
            moved = held[spot[i], plane - cx, here, :]
        else:
            moved = held[spot[i], plane - cx, pl.ds(PAD + first - cz, rows), :]
        if cy != 0:
            moved = pltpu.roll(moved, cy % lanes, 1)
        fluid = source_z[cz] >= walls[1 + cy, plane - cx]
        g[i] = jnp.where(fluid, moved, post[opposite(i)])
    return g


def kernel(n, rows, pops, heights, stage, last_post, other_post, walls, ground, ground_sem, in_sem, sent_up, sent_down, got_up, got_down, wall_sem):
    width, depth, lanes = pops.shape[1], pops.shape[2], pops.shape[3]
    chunks = depth // rows
    even_post, odd_post = (other_post, last_post) if STEPS % 2 == 0 else (last_post, other_post)
    me = lax.axis_index("gx")
    right, left = lax.rem(me + 1, n), lax.rem(me + n - 1, n)
    edges = [1, width] if width > 1 else [1]
    inner = list(range(2, width))

    fetches = {
        plane: pltpu.make_async_copy(pops.at[:, plane - 1], stage.at[:, plane - 1], in_sem.at[plane - 1])
        for plane in edges + inner
    }
    for plane in edges:
        fetches[plane].start()
    ground_fetch = pltpu.make_async_copy(heights, ground, ground_sem)
    ground_fetch.start()

    barrier = pltpu.get_barrier_semaphore()
    for neighbour in (left, right):
        pl.semaphore_signal(barrier, inc=1, device_id={"gx": neighbour}, device_id_type=MESH)

    wall_up = pltpu.make_async_remote_copy(
        walls.at[1, width], walls.at[1, 0], wall_sem.at[0], wall_sem.at[1], device_id={"gx": right}, device_id_type=MESH)
    wall_down = pltpu.make_async_remote_copy(
        walls.at[1, 1], walls.at[1, width + 1], wall_sem.at[2], wall_sem.at[3], device_id={"gx": left}, device_id_type=MESH)

    def copies(held, step, chunk):
        span = pl.ds(pl.multiple_of(PAD + chunk * rows, 8), rows)
        up = pltpu.make_async_remote_copy(
            held.at[pl.ds(0, MOVING), width, span], held.at[pl.ds(0, MOVING), 0, span],
            sent_up.at[step, chunk], got_up.at[step, chunk], device_id={"gx": right}, device_id_type=MESH)
        down = pltpu.make_async_remote_copy(
            held.at[pl.ds(MOVING, MOVING), 1, span], held.at[pl.ds(MOVING, MOVING), width + 1, span],
            sent_down.at[step, chunk], got_down.at[step, chunk], device_id={"gx": left}, device_id_type=MESH)
        return up, down

    def arrived(held, step, chunk):
        for copy in copies(held, step, chunk):
            copy.wait_recv()

    def left_here(held, step, chunk):
        for copy in copies(held, step, chunk):
            copy.wait_send()

    def keep_post(held, first, posts):
        span = pl.ds(pl.multiple_of(PAD + first, 8), rows)
        for plane, post in posts.items():
            for i in range(19):
                held[spot[i], plane, span, :] = post[i]

    stream_here = functools.partial(stream, walls, rows, depth)

    def first_post(planes, chunk):
        first = chunk * rows
        span = pl.ds(pl.multiple_of(first, 8), rows)
        keep_post(even_post, first, {
            plane: collide({i: stage[i, plane - 1, span, :] for i in range(19)}) for plane in planes
        })

    for plane in edges:
        fetches[plane].wait()
    for plane in inner:
        fetches[plane].start()
    first_post(edges, 0)
    pl.semaphore_wait(barrier, 2)
    for copy in copies(even_post, 0, 0):
        copy.start()
    ground_fetch.wait()
    for plane in range(1, width + 1):
        walls[1, plane] = jnp.broadcast_to(ground[plane - 1 : plane, :], (rows, lanes))
    wall_up.start()
    wall_down.start()

    def first_chunk(chunk, carry):
        first_post(edges, chunk)
        for copy in copies(even_post, 0, chunk):
            copy.start()
        return carry

    lax.fori_loop(1, chunks, first_chunk, 0)
    for plane in inner:
        fetches[plane].wait()

    def first_inner(chunk, carry):
        first_post(inner, chunk)
        return carry

    lax.fori_loop(0, chunks, first_inner, 0)

    wall_up.wait()
    wall_down.wait()
    for plane in range(width + 2):
        for cy in (1, -1):
            walls[1 + cy, plane] = pltpu.roll(walls[1, plane], cy % lanes, 1)

    def one_step(step, before, held):
        arrived(before, step - 1, 0)

        def one_chunk(chunk, inside):
            first = chunk * rows

            @pl.when(chunk < chunks - 1)
            def _():
                arrived(before, step - 1, chunk + 1)

            @pl.when(step >= 2)
            def _():
                left_here(held, step - 2, chunk)

            keep_post(held, first, {plane: collide(stream_here(before, plane, first)) for plane in edges})
            for copy in copies(held, step, chunk):
                copy.start()
            keep_post(held, first, {plane: collide(stream_here(before, plane, first)) for plane in inner})
            return inside

        lax.fori_loop(0, chunks, one_chunk, 0)

    def two_steps(pair, carry):
        one_step(2 * pair + 1, even_post, odd_post)
        one_step(2 * pair + 2, odd_post, even_post)
        return carry

    lax.fori_loop(0, (STEPS - 1) // 2, two_steps, 0)
    if STEPS % 2 == 0:
        one_step(STEPS - 1, even_post, odd_post)

    def last_inner(chunk, carry):
        first = chunk * rows
        span = pl.ds(pl.multiple_of(first, 8), rows)
        streamed = {plane: stream_here(last_post, plane, first) for plane in inner}
        for plane, g in streamed.items():
            for i in range(19):
                stage[i, plane - 1, span, :] = g[i]
        return carry

    lax.fori_loop(0, chunks, last_inner, 0)
    arrived(last_post, STEPS - 1, 0)

    def last_edges(chunk, carry):
        first = chunk * rows
        span = pl.ds(pl.multiple_of(first, 8), rows)

        @pl.when(chunk < chunks - 1)
        def _():
            arrived(last_post, STEPS - 1, chunk + 1)

        streamed = {plane: stream_here(last_post, plane, first) for plane in edges}
        for plane, g in streamed.items():
            for i in range(19):
                stage[i, plane - 1, span, :] = g[i]
        return carry

    lax.fori_loop(0, chunks, last_edges, 0)

    def finish(chunk, carry):
        left_here(other_post, STEPS - 2, chunk)
        left_here(last_post, STEPS - 1, chunk)
        return carry

    lax.fori_loop(0, chunks, finish, 0)


def write_kernel(stage, out, sem):
    copies = [
        pltpu.make_async_copy(stage.at[:, plane], out.at[:, plane], sem.at[plane]) for plane in range(stage.shape[1])
    ]
    for copy in copies:
        copy.start()
    for copy in copies:
        copy.wait()


def solution(mesh):
    n = mesh.shape["gx"]

    def per_device(pops, heights):
        kinds, width, depth, lanes = pops.shape
        rows = 16 if depth % 16 == 0 else 8
        chunks = depth // rows
        dma = pltpu.SemaphoreType.DMA
        held_shape = (kinds, width + 2, depth + 2 * PAD, lanes)
        wall_shape = (3, width + 2, rows, lanes)
        hbm, vmem = pl.BlockSpec(memory_space=pltpu.HBM), pl.BlockSpec(memory_space=pltpu.VMEM)
        kept = pl.pallas_call(
            functools.partial(kernel, n, rows),
            out_shape=pltpu.VMEM(pops.shape, jnp.float32),
            in_specs=[hbm] * 2,
            out_specs=vmem,
            scratch_shapes=[
                pltpu.VMEM(held_shape, jnp.float32),
                pltpu.VMEM(held_shape, jnp.float32),
                pltpu.VMEM(wall_shape, jnp.int32),
                pltpu.VMEM(heights.shape, jnp.int32),
                dma,
                dma((width,)),
                dma((STEPS, chunks)),
                dma((STEPS, chunks)),
                dma((STEPS, chunks)),
                dma((STEPS, chunks)),
                dma((4,)),
            ],
            compiler_params=pltpu.CompilerParams(
                collective_id=0, has_side_effects=True, vmem_limit_bytes=60 * 1024 * 1024
            ),
            cost_estimate=pl.CostEstimate(
                flops=250 * STEPS * width * depth * lanes, bytes_accessed=4 * pops.size, transcendentals=0
            ),
        )(pops, heights)
        return pl.pallas_call(
            write_kernel,
            out_shape=pltpu.HBM(pops.shape, jnp.float32),
            in_specs=[vmem],
            out_specs=hbm,
            scratch_shapes=[dma((width,))],
            compiler_params=pltpu.CompilerParams(vmem_limit_bytes=32 * 1024 * 1024),
            cost_estimate=pl.CostEstimate(flops=0, bytes_accessed=4 * pops.size, transcendentals=0),
        )(kept)

    return jax.shard_map(
        per_device,
        mesh=mesh,
        in_specs=(P(None, ("dir", "gx"), None, None), P(("dir", "gx"), None)),
        out_specs=P(None, ("dir", "gx"), None, None),
        check_vma=False,
    )
```

```python
import functools

import jax
import jax.numpy as jnp
from jax import lax
from jax.experimental import pallas as pl
from jax.experimental.pallas import tpu as pltpu
from jax.sharding import PartitionSpec as P

STEPS = 6
PAD = 8
MESH = pl.DeviceIdType.MESH

velocity_table = [
    (0, 0, 0),
    (1, 0, 0),
    (-1, 0, 0),
    (0, 1, 0),
    (0, -1, 0),
    (0, 0, 1),
    (0, 0, -1),
    (1, 1, 0),
    (-1, -1, 0),
    (1, -1, 0),
    (-1, 1, 0),
    (1, 0, 1),
    (-1, 0, -1),
    (1, 0, -1),
    (-1, 0, 1),
    (0, 1, 1),
    (0, -1, -1),
    (0, 1, -1),
    (0, -1, 1),
]
omega_rate = 1.9
held_order = [1, 7, 9, 11, 13, 2, 8, 10, 12, 14, 0, 3, 4, 5, 6, 15, 16, 17, 18]
spot = {component: place for place, component in enumerate(held_order)}
MOVING = 5


def opposite(component):
    if component == 0:
        return 0
    return component + 1 if component % 2 == 1 else component - 1


def collide(g):
    sums = {i: g[i] + g[i + 1] for i in range(1, 19, 2)}
    diffs = {i: g[i] - g[i + 1] for i in range(1, 19, 2)}
    axis_sum = sums[1] + sums[3] + sums[5]
    cross_sum = (sums[7] + sums[9]) + (sums[11] + sums[13]) + (sums[15] + sums[17])
    total = 12.0 * g[0] + 2.0 * axis_sum + cross_sum
    scale = 3.0 * omega_rate / 36.0
    nx = scale * (2.0 * diffs[1] + ((diffs[7] + diffs[9]) + (diffs[11] + diffs[13])))
    ny = scale * (2.0 * diffs[3] + ((diffs[7] - diffs[9]) + (diffs[15] + diffs[17])))
    nz = scale * (2.0 * diffs[5] + ((diffs[11] - diffs[13]) + (diffs[15] - diffs[17])))
    k = (omega_rate * 4.5 / 36.0 / (scale * scale)) / total
    base = (omega_rate / 36.0) * total - (k * (1.0 / 3.0)) * (nx * nx + ny * ny + nz * nz)
    along = {1: nx, 3: ny, 5: nz, 7: nx + ny, 9: nx - ny, 11: nx + nz, 13: nx - nz, 15: ny + nz, 17: ny - nz}
    keep = 1.0 - omega_rate
    post = {0: base + keep * g[0]}
    for i, t in along.items():
        even = base + k * (t * t)
        post[i] = (even + t) + keep * g[i]
        post[i + 1] = (even - t) + keep * g[i + 1]
    return post


def stream(walls, rows, depth, held, plane, first):
    lanes = held.shape[-1]
    z = lax.broadcasted_iota(jnp.int32, (rows, lanes), 0) + first
    source_z = {0: z, 1: z - 1, -1: jnp.where(z == depth - 1, -1, z + 1)}
    here = pl.ds(pl.multiple_of(PAD + first, 8), rows)
    post = {i: held[spot[i], plane, here, :] for i in range(19)}
    g = {}
    for i in range(19):
        cx, cy, cz = velocity_table[i]
        if cx == 0 and cz == 0:
            moved = post[i]
        elif cz == 0:
            moved = held[spot[i], plane - cx, here, :]
        else:
            moved = held[spot[i], plane - cx, pl.ds(PAD + first - cz, rows), :]
        if cy != 0:
            moved = pltpu.roll(moved, cy % lanes, 1)
        fluid = source_z[cz] >= walls[1 + cy, plane - cx]
        g[i] = jnp.where(fluid, moved, post[opposite(i)])
    return g


def kernel(n, rows, pops, heights, last_post, walls, stage, other_post, ground, ground_sem, in_sem, sent_up, sent_down, got_up, got_down, wall_sem):
    width, depth, lanes = pops.shape[1], pops.shape[2], pops.shape[3]
    chunks = depth // rows
    even_post, odd_post = (other_post, last_post) if STEPS % 2 == 0 else (last_post, other_post)
    me = lax.axis_index("gx")
    right, left = lax.rem(me + 1, n), lax.rem(me + n - 1, n)
    edges = [1, width] if width > 1 else [1]
    inner = list(range(2, width))

    fetches = {
        plane: pltpu.make_async_copy(pops.at[:, plane - 1], stage.at[:, plane - 1], in_sem.at[plane - 1])
        for plane in edges + inner
    }
    for plane in edges:
        fetches[plane].start()
    ground_fetch = pltpu.make_async_copy(heights, ground, ground_sem)
    ground_fetch.start()

    barrier = pltpu.get_barrier_semaphore()
    for neighbour in (left, right):
        pl.semaphore_signal(barrier, inc=1, device_id={"gx": neighbour}, device_id_type=MESH)

    wall_up = pltpu.make_async_remote_copy(
        walls.at[1, width], walls.at[1, 0], wall_sem.at[0], wall_sem.at[1], device_id={"gx": right}, device_id_type=MESH)
    wall_down = pltpu.make_async_remote_copy(
        walls.at[1, 1], walls.at[1, width + 1], wall_sem.at[2], wall_sem.at[3], device_id={"gx": left}, device_id_type=MESH)

    def copies(held, step, chunk):
        span = pl.ds(pl.multiple_of(PAD + chunk * rows, 8), rows)
        up = pltpu.make_async_remote_copy(
            held.at[pl.ds(0, MOVING), width, span], held.at[pl.ds(0, MOVING), 0, span],
            sent_up.at[step, chunk], got_up.at[step, chunk], device_id={"gx": right}, device_id_type=MESH)
        down = pltpu.make_async_remote_copy(
            held.at[pl.ds(MOVING, MOVING), 1, span], held.at[pl.ds(MOVING, MOVING), width + 1, span],
            sent_down.at[step, chunk], got_down.at[step, chunk], device_id={"gx": left}, device_id_type=MESH)
        return up, down

    def arrived(held, step, chunk):
        for copy in copies(held, step, chunk):
            copy.wait_recv()

    def left_here(held, step, chunk):
        for copy in copies(held, step, chunk):
            copy.wait_send()

    def keep_post(held, first, posts):
        span = pl.ds(pl.multiple_of(PAD + first, 8), rows)
        for plane, post in posts.items():
            for i in range(19):
                held[spot[i], plane, span, :] = post[i]

    stream_here = functools.partial(stream, walls, rows, depth)

    def first_post(planes, chunk):
        first = chunk * rows
        span = pl.ds(pl.multiple_of(first, 8), rows)
        keep_post(even_post, first, {
            plane: collide({i: stage[i, plane - 1, span, :] for i in range(19)}) for plane in planes
        })

    for plane in edges:
        fetches[plane].wait()
    for plane in inner:
        fetches[plane].start()
    first_post(edges, 0)
    pl.semaphore_wait(barrier, 2)
    for copy in copies(even_post, 0, 0):
        copy.start()
    ground_fetch.wait()
    for plane in range(1, width + 1):
        walls[1, plane] = jnp.broadcast_to(ground[plane - 1 : plane, :], (rows, lanes))
    wall_up.start()
    wall_down.start()

    def first_chunk(chunk, carry):
        first_post(edges, chunk)
        for copy in copies(even_post, 0, chunk):
            copy.start()
        return carry

    lax.fori_loop(1, chunks, first_chunk, 0)
    for plane in inner:
        fetches[plane].wait()

    def first_inner(chunk, carry):
        first_post(inner, chunk)
        return carry

    lax.fori_loop(0, chunks, first_inner, 0)

    wall_up.wait()
    wall_down.wait()
    for plane in range(width + 2):
        for cy in (1, -1):
            walls[1 + cy, plane] = pltpu.roll(walls[1, plane], cy % lanes, 1)

    def one_step(step, before, held):
        arrived(before, step - 1, 0)

        def one_chunk(chunk, inside):
            first = chunk * rows

            @pl.when(chunk < chunks - 1)
            def _():
                arrived(before, step - 1, chunk + 1)

            keep_post(held, first, {plane: collide(stream_here(before, plane, first)) for plane in edges})
            for copy in copies(held, step, chunk):
                copy.start()
            keep_post(held, first, {plane: collide(stream_here(before, plane, first)) for plane in inner})
            left_here(before, step - 1, chunk)
            return inside

        lax.fori_loop(0, chunks, one_chunk, 0)

    def two_steps(pair, carry):
        one_step(2 * pair + 1, even_post, odd_post)
        one_step(2 * pair + 2, odd_post, even_post)
        return carry

    lax.fori_loop(0, (STEPS - 1) // 2, two_steps, 0)
    if STEPS % 2 == 0:
        one_step(STEPS - 1, even_post, odd_post)

    def last_inner(chunk, carry):
        first = chunk * rows
        span = pl.ds(pl.multiple_of(first, 8), rows)
        streamed = {plane: stream_here(last_post, plane, first) for plane in inner}
        for plane, g in streamed.items():
            for i in range(19):
                stage[i, plane - 1, span, :] = g[i]
        return carry

    lax.fori_loop(0, chunks, last_inner, 0)

    def finish(chunk, carry):
        left_here(last_post, STEPS - 1, chunk)
        arrived(last_post, STEPS - 1, chunk)
        return carry

    lax.fori_loop(0, chunks, finish, 0)


def last_kernel(rows, last_post, walls, stage, out, ends, inner_sem, out_sem):
    width, depth = stage.shape[1], stage.shape[2]
    chunks = depth // rows
    edges = [1, width] if width > 1 else [1]
    inner_copies = [
        pltpu.make_async_copy(stage.at[:, plane - 1], out.at[:, plane - 1], inner_sem.at[plane - 1])
        for plane in range(2, width)
    ]
    for copy in inner_copies:
        copy.start()

    def write_back(chunk):
        span = pl.ds(pl.multiple_of(chunk * rows, 8), rows)
        return [
            pltpu.make_async_copy(ends.at[:, place, span], out.at[:, plane - 1, span], out_sem.at[chunk, place])
            for place, plane in enumerate(edges)
        ]

    def one_chunk(chunk, carry):
        first = chunk * rows
        span = pl.ds(pl.multiple_of(first, 8), rows)
        streamed = [stream(walls, rows, depth, last_post, plane, first) for plane in edges]
        for place, g in enumerate(streamed):
            for i in range(19):
                ends[i, place, span, :] = g[i]
        for copy in write_back(chunk):
            copy.start()
        return carry

    lax.fori_loop(0, chunks, one_chunk, 0)

    def finish(chunk, carry):
        for copy in write_back(chunk):
            copy.wait()
        return carry

    lax.fori_loop(0, chunks, finish, 0)
    for copy in inner_copies:
        copy.wait()


def solution(mesh):
    n = mesh.shape["gx"]

    def per_device(pops, heights):
        kinds, width, depth, lanes = pops.shape
        rows = 8
        chunks = depth // rows
        dma = pltpu.SemaphoreType.DMA
        held_shape = (kinds, width + 2, depth + 2 * PAD, lanes)
        wall_shape = (3, width + 2, rows, lanes)
        hbm, vmem = pl.BlockSpec(memory_space=pltpu.HBM), pl.BlockSpec(memory_space=pltpu.VMEM)
        kept = pl.pallas_call(
            functools.partial(kernel, n, rows),
            out_shape=[
                pltpu.VMEM(held_shape, jnp.float32),
                pltpu.VMEM(wall_shape, jnp.int32),
                pltpu.VMEM(pops.shape, jnp.float32),
            ],
            in_specs=[hbm] * 2,
            out_specs=[vmem] * 3,
            scratch_shapes=[
                pltpu.VMEM(held_shape, jnp.float32),
                pltpu.VMEM(heights.shape, jnp.int32),
                dma,
                dma((width,)),
                dma((STEPS, chunks)),
                dma((STEPS, chunks)),
                dma((STEPS, chunks)),
                dma((STEPS, chunks)),
                dma((4,)),
            ],
            compiler_params=pltpu.CompilerParams(
                collective_id=0, has_side_effects=True, vmem_limit_bytes=55 * 1024 * 1024
            ),
            cost_estimate=pl.CostEstimate(
                flops=250 * STEPS * width * depth * lanes, bytes_accessed=4 * pops.size, transcendentals=0
            ),
        )(pops, heights)
        return pl.pallas_call(
            functools.partial(last_kernel, rows),
            out_shape=jax.ShapeDtypeStruct(pops.shape, pops.dtype),
            in_specs=[vmem] * 3,
            out_specs=hbm,
            scratch_shapes=[
                pltpu.VMEM((kinds, min(width, 2), depth, lanes), jnp.float32),
                dma((width,)),
                dma((chunks, 2)),
            ],
            compiler_params=pltpu.CompilerParams(vmem_limit_bytes=32 * 1024 * 1024),
            cost_estimate=pl.CostEstimate(flops=20 * pops.size, bytes_accessed=4 * pops.size, transcendentals=0),
        )(*kept)

    return jax.shard_map(
        per_device,
        mesh=mesh,
        in_specs=(P(None, ("dir", "gx"), None, None), P(("dir", "gx"), None)),
        out_specs=P(None, ("dir", "gx"), None, None),
        check_vma=False,
    )
```

```python
import functools

import jax
import jax.numpy as jnp
from jax import lax
from jax.experimental import pallas as pl
from jax.experimental.pallas import tpu as pltpu
from jax.sharding import PartitionSpec as P

STEPS = 6
PAD = 8
MESH = pl.DeviceIdType.MESH

velocity_table = [
    (0, 0, 0),
    (1, 0, 0),
    (-1, 0, 0),
    (0, 1, 0),
    (0, -1, 0),
    (0, 0, 1),
    (0, 0, -1),
    (1, 1, 0),
    (-1, -1, 0),
    (1, -1, 0),
    (-1, 1, 0),
    (1, 0, 1),
    (-1, 0, -1),
    (1, 0, -1),
    (-1, 0, 1),
    (0, 1, 1),
    (0, -1, -1),
    (0, 1, -1),
    (0, -1, 1),
]
omega_rate = 1.9
held_order = [1, 7, 9, 11, 13, 2, 8, 10, 12, 14, 0, 3, 4, 5, 6, 15, 16, 17, 18]
spot = {component: place for place, component in enumerate(held_order)}
MOVING = 5


def opposite(component):
    if component == 0:
        return 0
    return component + 1 if component % 2 == 1 else component - 1


def collide(g):
    sums = {i: g[i] + g[i + 1] for i in range(1, 19, 2)}
    diffs = {i: g[i] - g[i + 1] for i in range(1, 19, 2)}
    axis_sum = sums[1] + sums[3] + sums[5]
    cross_sum = (sums[7] + sums[9]) + (sums[11] + sums[13]) + (sums[15] + sums[17])
    total = 12.0 * g[0] + 2.0 * axis_sum + cross_sum
    scale = 3.0 * omega_rate / 36.0
    nx = scale * (2.0 * diffs[1] + ((diffs[7] + diffs[9]) + (diffs[11] + diffs[13])))
    ny = scale * (2.0 * diffs[3] + ((diffs[7] - diffs[9]) + (diffs[15] + diffs[17])))
    nz = scale * (2.0 * diffs[5] + ((diffs[11] - diffs[13]) + (diffs[15] - diffs[17])))
    k = (omega_rate * 4.5 / 36.0 / (scale * scale)) / total
    base = (omega_rate / 36.0) * total - (k * (1.0 / 3.0)) * (nx * nx + ny * ny + nz * nz)
    along = {1: nx, 3: ny, 5: nz, 7: nx + ny, 9: nx - ny, 11: nx + nz, 13: nx - nz, 15: ny + nz, 17: ny - nz}
    keep = 1.0 - omega_rate
    post = {0: base + keep * g[0]}
    for i, t in along.items():
        even = base + k * (t * t)
        post[i] = (even + t) + keep * g[i]
        post[i + 1] = (even - t) + keep * g[i + 1]
    return post


def stream(walls, rows, depth, held, plane, first):
    lanes = held.shape[-1]
    z = lax.broadcasted_iota(jnp.int32, (rows, lanes), 0) + first
    source_z = {0: z, 1: z - 1, -1: jnp.where(z == depth - 1, -1, z + 1)}
    here = pl.ds(pl.multiple_of(PAD + first, 8), rows)
    post = {i: held[spot[i], plane, here, :] for i in range(19)}
    g = {}
    for i in range(19):
        cx, cy, cz = velocity_table[i]
        if cx == 0 and cz == 0:
            moved = post[i]
        elif cz == 0:
            moved = held[spot[i], plane - cx, here, :]
        else:
            moved = held[spot[i], plane - cx, pl.ds(PAD + first - cz, rows), :]
        if cy != 0:
            moved = pltpu.roll(moved, cy % lanes, 1)
        fluid = source_z[cz] >= walls[1 + cy, plane - cx]
        g[i] = jnp.where(fluid, moved, post[opposite(i)])
    return g


def kernel(n, rows, pops, heights, last_post, walls, stage, other_post, ground, ground_sem, in_sem, sent_up, sent_down, got_up, got_down, wall_sem):
    width, depth, lanes = pops.shape[1], pops.shape[2], pops.shape[3]
    chunks = depth // rows
    even_post, odd_post = (other_post, last_post) if STEPS % 2 == 0 else (last_post, other_post)
    me = lax.axis_index("gx")
    right, left = lax.rem(me + 1, n), lax.rem(me + n - 1, n)
    edges = [1, width] if width > 1 else [1]
    inner = list(range(2, width))

    fetches = {
        plane: pltpu.make_async_copy(pops.at[:, plane - 1], stage.at[:, plane - 1], in_sem.at[plane - 1])
        for plane in edges + inner
    }
    for place, plane in enumerate(edges):
        fetches[plane].start(priority=place % 2)
    ground_fetch = pltpu.make_async_copy(heights, ground, ground_sem)
    ground_fetch.start()

    barrier = pltpu.get_barrier_semaphore()
    for neighbour in (left, right):
        pl.semaphore_signal(barrier, inc=1, device_id={"gx": neighbour}, device_id_type=MESH)

    wall_up = pltpu.make_async_remote_copy(
        walls.at[1, width], walls.at[1, 0], wall_sem.at[0], wall_sem.at[1], device_id={"gx": right}, device_id_type=MESH)
    wall_down = pltpu.make_async_remote_copy(
        walls.at[1, 1], walls.at[1, width + 1], wall_sem.at[2], wall_sem.at[3], device_id={"gx": left}, device_id_type=MESH)

    def copies(held, step, chunk):
        span = pl.ds(pl.multiple_of(PAD + chunk * rows, 8), rows)
        up = pltpu.make_async_remote_copy(
            held.at[pl.ds(0, MOVING), width, span], held.at[pl.ds(0, MOVING), 0, span],
            sent_up.at[step, chunk], got_up.at[step, chunk], device_id={"gx": right}, device_id_type=MESH)
        down = pltpu.make_async_remote_copy(
            held.at[pl.ds(MOVING, MOVING), 1, span], held.at[pl.ds(MOVING, MOVING), width + 1, span],
            sent_down.at[step, chunk], got_down.at[step, chunk], device_id={"gx": left}, device_id_type=MESH)
        return up, down

    def arrived(held, step, chunk):
        for copy in copies(held, step, chunk):
            copy.wait_recv()

    def left_here(held, step, chunk):
        for copy in copies(held, step, chunk):
            copy.wait_send()

    def keep_post(held, first, posts):
        span = pl.ds(pl.multiple_of(PAD + first, 8), rows)
        for plane, post in posts.items():
            for i in range(19):
                held[spot[i], plane, span, :] = post[i]

    stream_here = functools.partial(stream, walls, rows, depth)

    def first_post(planes, chunk):
        first = chunk * rows
        span = pl.ds(pl.multiple_of(first, 8), rows)
        keep_post(even_post, first, {
            plane: collide({i: stage[i, plane - 1, span, :] for i in range(19)}) for plane in planes
        })

    for plane in edges:
        fetches[plane].wait()
    for place, plane in enumerate(inner):
        fetches[plane].start(priority=place % 2)
    first_post(edges, 0)
    pl.semaphore_wait(barrier, 2)
    for copy in copies(even_post, 0, 0):
        copy.start()
    ground_fetch.wait()
    for plane in range(1, width + 1):
        walls[1, plane] = jnp.broadcast_to(ground[plane - 1 : plane, :], (rows, lanes))
    wall_up.start()
    wall_down.start()

    def first_chunk(chunk, carry):
        first_post(edges, chunk)
        for copy in copies(even_post, 0, chunk):
            copy.start()
        return carry

    lax.fori_loop(1, chunks, first_chunk, 0)
    for plane in inner:
        fetches[plane].wait()

    def first_inner(chunk, carry):
        first_post(inner, chunk)
        return carry

    lax.fori_loop(0, chunks, first_inner, 0)

    wall_up.wait()
    wall_down.wait()
    for plane in range(width + 2):
        for cy in (1, -1):
            walls[1 + cy, plane] = pltpu.roll(walls[1, plane], cy % lanes, 1)

    def one_step(step, before, held):
        arrived(before, step - 1, 0)

        def one_chunk(chunk, inside):
            first = chunk * rows

            @pl.when(chunk < chunks - 1)
            def _():
                arrived(before, step - 1, chunk + 1)

            keep_post(held, first, {plane: collide(stream_here(before, plane, first)) for plane in edges})
            for copy in copies(held, step, chunk):
                copy.start()
            keep_post(held, first, {plane: collide(stream_here(before, plane, first)) for plane in inner})
            left_here(before, step - 1, chunk)
            return inside

        lax.fori_loop(0, chunks, one_chunk, 0)

    def two_steps(pair, carry):
        one_step(2 * pair + 1, even_post, odd_post)
        one_step(2 * pair + 2, odd_post, even_post)
        return carry

    lax.fori_loop(0, (STEPS - 1) // 2, two_steps, 0)
    if STEPS % 2 == 0:
        one_step(STEPS - 1, even_post, odd_post)

    def last_inner(chunk, carry):
        first = chunk * rows
        span = pl.ds(pl.multiple_of(first, 8), rows)
        streamed = {plane: stream_here(last_post, plane, first) for plane in inner}
        for plane, g in streamed.items():
            for i in range(19):
                stage[i, plane - 1, span, :] = g[i]
        return carry

    lax.fori_loop(0, chunks, last_inner, 0)

    def finish(chunk, carry):
        left_here(last_post, STEPS - 1, chunk)
        arrived(last_post, STEPS - 1, chunk)
        return carry

    lax.fori_loop(0, chunks, finish, 0)


def last_kernel(rows, last_post, walls, stage, out, ends, inner_sem, out_sem):
    width, depth = stage.shape[1], stage.shape[2]
    chunks = depth // rows
    edges = [1, width] if width > 1 else [1]
    inner_copies = [
        pltpu.make_async_copy(stage.at[:, plane - 1], out.at[:, plane - 1], inner_sem.at[plane - 1])
        for plane in range(2, width)
    ]
    for place, copy in enumerate(inner_copies):
        copy.start(priority=place % 2)

    def write_back(chunk):
        span = pl.ds(pl.multiple_of(chunk * rows, 8), rows)
        return [
            pltpu.make_async_copy(ends.at[:, place, span], out.at[:, plane - 1, span], out_sem.at[chunk, place])
            for place, plane in enumerate(edges)
        ]

    def one_chunk(chunk, carry):
        first = chunk * rows
        span = pl.ds(pl.multiple_of(first, 8), rows)
        streamed = [stream(walls, rows, depth, last_post, plane, first) for plane in edges]
        for place, g in enumerate(streamed):
            for i in range(19):
                ends[i, place, span, :] = g[i]
        for place, copy in enumerate(write_back(chunk)):
            copy.start(priority=place)
        return carry

    lax.fori_loop(0, chunks, one_chunk, 0)

    def finish(chunk, carry):
        for copy in write_back(chunk):
            copy.wait()
        return carry

    lax.fori_loop(0, chunks, finish, 0)
    for copy in inner_copies:
        copy.wait()


def solution(mesh):
    n = mesh.shape["gx"]

    def per_device(pops, heights):
        kinds, width, depth, lanes = pops.shape
        rows = 8
        chunks = depth // rows
        dma = pltpu.SemaphoreType.DMA
        held_shape = (kinds, width + 2, depth + 2 * PAD, lanes)
        wall_shape = (3, width + 2, rows, lanes)
        hbm, vmem = pl.BlockSpec(memory_space=pltpu.HBM), pl.BlockSpec(memory_space=pltpu.VMEM)
        kept = pl.pallas_call(
            functools.partial(kernel, n, rows),
            out_shape=[
                pltpu.VMEM(held_shape, jnp.float32),
                pltpu.VMEM(wall_shape, jnp.int32),
                pltpu.VMEM(pops.shape, jnp.float32),
            ],
            in_specs=[hbm] * 2,
            out_specs=[vmem] * 3,
            scratch_shapes=[
                pltpu.VMEM(held_shape, jnp.float32),
                pltpu.VMEM(heights.shape, jnp.int32),
                dma,
                dma((width,)),
                dma((STEPS, chunks)),
                dma((STEPS, chunks)),
                dma((STEPS, chunks)),
                dma((STEPS, chunks)),
                dma((4,)),
            ],
            compiler_params=pltpu.CompilerParams(
                collective_id=0, has_side_effects=True, vmem_limit_bytes=55 * 1024 * 1024
            ),
            cost_estimate=pl.CostEstimate(
                flops=250 * STEPS * width * depth * lanes, bytes_accessed=4 * pops.size, transcendentals=0
            ),
        )(pops, heights)
        return pl.pallas_call(
            functools.partial(last_kernel, rows),
            out_shape=jax.ShapeDtypeStruct(pops.shape, pops.dtype),
            in_specs=[vmem] * 3,
            out_specs=hbm,
            scratch_shapes=[
                pltpu.VMEM((kinds, min(width, 2), depth, lanes), jnp.float32),
                dma((width,)),
                dma((chunks, 2)),
            ],
            compiler_params=pltpu.CompilerParams(vmem_limit_bytes=32 * 1024 * 1024),
            cost_estimate=pl.CostEstimate(flops=20 * pops.size, bytes_accessed=4 * pops.size, transcendentals=0),
        )(*kept)

    return jax.shard_map(
        per_device,
        mesh=mesh,
        in_specs=(P(None, ("dir", "gx"), None, None), P(("dir", "gx"), None)),
        out_specs=P(None, ("dir", "gx"), None, None),
        check_vma=False,
    )
```

```python
import functools

import jax
import jax.numpy as jnp
from jax import lax
from jax.experimental import pallas as pl
from jax.experimental.pallas import tpu as pltpu
from jax.sharding import PartitionSpec as P

STEPS = 6
PAD = 8
MESH = pl.DeviceIdType.MESH

velocity_table = [
    (0, 0, 0),
    (1, 0, 0),
    (-1, 0, 0),
    (0, 1, 0),
    (0, -1, 0),
    (0, 0, 1),
    (0, 0, -1),
    (1, 1, 0),
    (-1, -1, 0),
    (1, -1, 0),
    (-1, 1, 0),
    (1, 0, 1),
    (-1, 0, -1),
    (1, 0, -1),
    (-1, 0, 1),
    (0, 1, 1),
    (0, -1, -1),
    (0, 1, -1),
    (0, -1, 1),
]
omega_rate = 1.9
held_order = [1, 7, 9, 11, 13, 2, 8, 10, 12, 14, 0, 3, 4, 5, 6, 15, 16, 17, 18]
spot = {component: place for place, component in enumerate(held_order)}
MOVING = 5
RELAY = 3
LAG_UP, LAG_DOWN = 4, 3


def opposite(component):
    if component == 0:
        return 0
    return component + 1 if component % 2 == 1 else component - 1


def collide(g):
    sums = {i: g[i] + g[i + 1] for i in range(1, 19, 2)}
    diffs = {i: g[i] - g[i + 1] for i in range(1, 19, 2)}
    axis_sum = sums[1] + sums[3] + sums[5]
    cross_sum = (sums[7] + sums[9]) + (sums[11] + sums[13]) + (sums[15] + sums[17])
    total = 12.0 * g[0] + 2.0 * axis_sum + cross_sum
    scale = 3.0 * omega_rate / 36.0
    nx = scale * (2.0 * diffs[1] + ((diffs[7] + diffs[9]) + (diffs[11] + diffs[13])))
    ny = scale * (2.0 * diffs[3] + ((diffs[7] - diffs[9]) + (diffs[15] + diffs[17])))
    nz = scale * (2.0 * diffs[5] + ((diffs[11] - diffs[13]) + (diffs[15] - diffs[17])))
    k = (omega_rate * 4.5 / 36.0 / (scale * scale)) / total
    base = (omega_rate / 36.0) * total - (k * (1.0 / 3.0)) * (nx * nx + ny * ny + nz * nz)
    along = {1: nx, 3: ny, 5: nz, 7: nx + ny, 9: nx - ny, 11: nx + nz, 13: nx - nz, 15: ny + nz, 17: ny - nz}
    keep = 1.0 - omega_rate
    post = {0: base + keep * g[0]}
    for i, t in along.items():
        even = base + k * (t * t)
        post[i] = (even + t) + keep * g[i]
        post[i + 1] = (even - t) + keep * g[i + 1]
    return post


def stream(walls, rows, depth, held, plane, first):
    lanes = held.shape[-1]
    z = lax.broadcasted_iota(jnp.int32, (rows, lanes), 0) + first
    source_z = {0: z, 1: z - 1, -1: jnp.where(z == depth - 1, -1, z + 1)}
    here = pl.ds(pl.multiple_of(PAD + first, 8), rows)
    post = {i: held[spot[i], plane, here, :] for i in range(19)}
    g = {}
    for i in range(19):
        cx, cy, cz = velocity_table[i]
        if cx == 0 and cz == 0:
            moved = post[i]
        elif cz == 0:
            moved = held[spot[i], plane - cx, here, :]
        else:
            moved = held[spot[i], plane - cx, pl.ds(PAD + first - cz, rows), :]
        if cy != 0:
            moved = pltpu.roll(moved, cy % lanes, 1)
        fluid = source_z[cz] >= walls[1 + cy, plane - cx]
        g[i] = jnp.where(fluid, moved, post[opposite(i)])
    return g


def kernel(n, rows, pops, heights, last_post, walls, stage, other_post, ground, ground_sem, in_sem, sent_up, sent_down, got_up, got_down, wall_sem, *relay):
    width, depth, lanes = pops.shape[1], pops.shape[2], pops.shape[3]
    chunks = depth // rows
    even_post, odd_post = (other_post, last_post) if STEPS % 2 == 0 else (last_post, other_post)
    me = lax.axis_index("gx")
    right, left = lax.rem(me + 1, n), lax.rem(me + n - 1, n)
    edges = [1, width] if width > 1 else [1]
    inner = list(range(2, width))
    relayed = len(relay) > 0
    if relayed:
        (relay_up, relay_down, relay_got_up, relay_got_down, relay_sent_up, relay_sent_down) = relay

    fetches = {
        plane: pltpu.make_async_copy(pops.at[:, plane - 1], stage.at[:, plane - 1], in_sem.at[plane - 1])
        for plane in edges + inner
    }
    for plane in edges:
        fetches[plane].start()
    ground_fetch = pltpu.make_async_copy(heights, ground, ground_sem)
    ground_fetch.start()

    barrier = pltpu.get_barrier_semaphore()
    for neighbour in (left, right):
        pl.semaphore_signal(barrier, inc=1, device_id={"gx": neighbour}, device_id_type=MESH)
    if relayed:

        @pl.when(me == RELAY)
        def _():
            for end in (0, n - 1):
                pl.semaphore_signal(barrier, inc=1, device_id={"gx": end}, device_id_type=MESH)

        for end in (0, n - 1):

            @pl.when(me == end)
            def _():
                pl.semaphore_signal(barrier, inc=1, device_id={"gx": RELAY}, device_id_type=MESH)


    wall_up = pltpu.make_async_remote_copy(
        walls.at[1, width], walls.at[1, 0], wall_sem.at[0], wall_sem.at[1], device_id={"gx": right}, device_id_type=MESH)
    wall_down = pltpu.make_async_remote_copy(
        walls.at[1, 1], walls.at[1, width + 1], wall_sem.at[2], wall_sem.at[3], device_id={"gx": left}, device_id_type=MESH)

    def copies(held, step, chunk):
        span = pl.ds(pl.multiple_of(PAD + chunk * rows, 8), rows)
        up = pltpu.make_async_remote_copy(
            held.at[pl.ds(0, MOVING), width, span], held.at[pl.ds(0, MOVING), 0, span],
            sent_up.at[step, chunk], got_up.at[step, chunk], device_id={"gx": right}, device_id_type=MESH)
        down = pltpu.make_async_remote_copy(
            held.at[pl.ds(MOVING, MOVING), 1, span], held.at[pl.ds(MOVING, MOVING), width + 1, span],
            sent_down.at[step, chunk], got_down.at[step, chunk], device_id={"gx": left}, device_id_type=MESH)
        return up, down

    def relay_copies(held, step, chunk):
        span = pl.ds(pl.multiple_of(PAD + chunk * rows, 8), rows)
        part = pl.ds(pl.multiple_of(chunk * rows, 8), rows)
        to_up = pltpu.make_async_remote_copy(
            held.at[pl.ds(0, MOVING), width, span], relay_up.at[step, :, part],
            sent_up.at[step, chunk], relay_got_up.at[step, chunk], device_id={"gx": RELAY}, device_id_type=MESH)
        from_up = pltpu.make_async_remote_copy(
            relay_up.at[step, :, part], held.at[pl.ds(0, MOVING), 0, span],
            relay_sent_up.at[step, chunk], got_up.at[step, chunk], device_id={"gx": 0}, device_id_type=MESH)
        to_down = pltpu.make_async_remote_copy(
            held.at[pl.ds(MOVING, MOVING), 1, span], relay_down.at[step, :, part],
            sent_down.at[step, chunk], relay_got_down.at[step, chunk], device_id={"gx": RELAY}, device_id_type=MESH)
        from_down = pltpu.make_async_remote_copy(
            relay_down.at[step, :, part], held.at[pl.ds(MOVING, MOVING), width + 1, span],
            relay_sent_down.at[step, chunk], got_down.at[step, chunk], device_id={"gx": n - 1}, device_id_type=MESH)
        return to_up, from_up, to_down, from_down

    def send(held, step, chunk):
        up, down = copies(held, step, chunk)
        if not relayed:
            up.start()
            down.start()
            return
        to_up, _, to_down, _ = relay_copies(held, step, chunk)
        for copy, to_relay, end in ((up, to_up, n - 1), (down, to_down, 0)):
            pl.when(me != end)(copy.start)
            pl.when(me == end)(to_relay.start)

    def pass_on(held, before, step, chunk):
        def one(buffer, its_step, its_chunk, upward):
            to_up, from_up, to_down, from_down = relay_copies(buffer, its_step, its_chunk)
            came, leaves = (to_up, from_up) if upward else (to_down, from_down)
            came.wait_recv()
            leaves.start()

        for lag, upward in ((LAG_DOWN, False), (LAG_UP, True)):
            if held is not None:
                pl.when((me == RELAY) & (chunk >= lag))(lambda: one(held, step, chunk - lag, upward))
            if before is not None:
                pl.when((me == RELAY) & (chunk < lag))(
                    lambda: one(before, step - 1, chunk + chunks - lag, upward))

    def arrived(held, step, chunk):
        for copy in copies(held, step, chunk):
            copy.wait_recv()

    def left_here(held, step, chunk):
        for copy in copies(held, step, chunk):
            copy.wait_send()

    def keep_post(held, first, posts):
        span = pl.ds(pl.multiple_of(PAD + first, 8), rows)
        for plane, post in posts.items():
            for i in range(19):
                held[spot[i], plane, span, :] = post[i]

    stream_here = functools.partial(stream, walls, rows, depth)

    def first_post(planes, chunk):
        first = chunk * rows
        span = pl.ds(pl.multiple_of(first, 8), rows)
        keep_post(even_post, first, {
            plane: collide({i: stage[i, plane - 1, span, :] for i in range(19)}) for plane in planes
        })

    for plane in edges:
        fetches[plane].wait()
    for plane in inner:
        fetches[plane].start()
    first_post(edges, 0)
    if relayed:
        at_end = (me == 0) | (me == n - 1)
        for peers, where in ((4, me == RELAY), (3, at_end), (2, (me != RELAY) & ~at_end)):

            @pl.when(where)
            def _():
                pl.semaphore_wait(barrier, peers)

    else:
        pl.semaphore_wait(barrier, 2)
    send(even_post, 0, 0)
    ground_fetch.wait()
    for plane in range(1, width + 1):
        walls[1, plane] = jnp.broadcast_to(ground[plane - 1 : plane, :], (rows, lanes))
    wall_up.start()
    wall_down.start()

    def first_chunk(chunk, carry):
        first_post(edges, chunk)
        send(even_post, 0, chunk)
        return carry

    lax.fori_loop(1, chunks, first_chunk, 0)
    for plane in inner:
        fetches[plane].wait()

    def first_inner(chunk, carry):
        if relayed:
            pass_on(even_post, None, 0, chunk)
        first_post(inner, chunk)
        return carry

    lax.fori_loop(0, chunks, first_inner, 0)

    wall_up.wait()
    wall_down.wait()
    for plane in range(width + 2):
        for cy in (1, -1):
            walls[1 + cy, plane] = pltpu.roll(walls[1, plane], cy % lanes, 1)

    def one_step(step, before, held):
        arrived(before, step - 1, 0)

        def one_chunk(chunk, inside):
            first = chunk * rows

            @pl.when(chunk < chunks - 1)
            def _():
                arrived(before, step - 1, chunk + 1)

            keep_post(held, first, {plane: collide(stream_here(before, plane, first)) for plane in edges})
            send(held, step, chunk)
            if relayed:
                pass_on(held, before, step, chunk)
            keep_post(held, first, {plane: collide(stream_here(before, plane, first)) for plane in inner})
            left_here(before, step - 1, chunk)
            return inside

        lax.fori_loop(0, chunks, one_chunk, 0)

    def two_steps(pair, carry):
        one_step(2 * pair + 1, even_post, odd_post)
        one_step(2 * pair + 2, odd_post, even_post)
        return carry

    lax.fori_loop(0, (STEPS - 1) // 2, two_steps, 0)
    if STEPS % 2 == 0:
        one_step(STEPS - 1, even_post, odd_post)

    def last_inner(chunk, carry):
        if relayed:
            pass_on(None, last_post, STEPS, chunk)
        first = chunk * rows
        span = pl.ds(pl.multiple_of(first, 8), rows)
        streamed = {plane: stream_here(last_post, plane, first) for plane in inner}
        for plane, g in streamed.items():
            for i in range(19):
                stage[i, plane - 1, span, :] = g[i]
        return carry

    lax.fori_loop(0, chunks, last_inner, 0)

    def finish(chunk, carry):
        left_here(last_post, STEPS - 1, chunk)
        arrived(last_post, STEPS - 1, chunk)
        return carry

    lax.fori_loop(0, chunks, finish, 0)
    if relayed:

        @pl.when(me == RELAY)
        def _():
            def passed(k, carry):
                _, from_up, _, from_down = relay_copies(last_post, k // chunks, k % chunks)
                from_up.wait_send()
                from_down.wait_send()
                return carry

            lax.fori_loop(0, STEPS * chunks, passed, 0)


def last_kernel(rows, last_post, walls, stage, out, ends, inner_sem, out_sem):
    width, depth = stage.shape[1], stage.shape[2]
    chunks = depth // rows
    edges = [1, width] if width > 1 else [1]
    inner_copies = [
        pltpu.make_async_copy(stage.at[:, plane - 1], out.at[:, plane - 1], inner_sem.at[plane - 1])
        for plane in range(2, width)
    ]
    for copy in inner_copies:
        copy.start()

    def write_back(chunk):
        span = pl.ds(pl.multiple_of(chunk * rows, 8), rows)
        return [
            pltpu.make_async_copy(ends.at[:, place, span], out.at[:, plane - 1, span], out_sem.at[chunk, place])
            for place, plane in enumerate(edges)
        ]

    def one_chunk(chunk, carry):
        first = chunk * rows
        span = pl.ds(pl.multiple_of(first, 8), rows)
        streamed = [stream(walls, rows, depth, last_post, plane, first) for plane in edges]
        for place, g in enumerate(streamed):
            for i in range(19):
                ends[i, place, span, :] = g[i]
        for copy in write_back(chunk):
            copy.start()
        return carry

    lax.fori_loop(0, chunks, one_chunk, 0)

    def finish(chunk, carry):
        for copy in write_back(chunk):
            copy.wait()
        return carry

    lax.fori_loop(0, chunks, finish, 0)
    for copy in inner_copies:
        copy.wait()


def solution(mesh):
    n = mesh.shape["gx"]

    def per_device(pops, heights):
        kinds, width, depth, lanes = pops.shape
        rows = 8
        chunks = depth // rows
        dma = pltpu.SemaphoreType.DMA
        held_shape = (kinds, width + 2, depth + 2 * PAD, lanes)
        wall_shape = (3, width + 2, rows, lanes)
        hbm, vmem = pl.BlockSpec(memory_space=pltpu.HBM), pl.BlockSpec(memory_space=pltpu.VMEM)
        relay = []
        if n >= 8 and chunks > max(LAG_UP, LAG_DOWN):
            relay = [pltpu.VMEM((STEPS, MOVING, depth, lanes), jnp.float32)] * 2 + [dma((STEPS, chunks))] * 4
        kept = pl.pallas_call(
            functools.partial(kernel, n, rows),
            out_shape=[
                pltpu.VMEM(held_shape, jnp.float32),
                pltpu.VMEM(wall_shape, jnp.int32),
                pltpu.VMEM(pops.shape, jnp.float32),
            ],
            in_specs=[hbm] * 2,
            out_specs=[vmem] * 3,
            scratch_shapes=[
                pltpu.VMEM(held_shape, jnp.float32),
                pltpu.VMEM(heights.shape, jnp.int32),
                dma,
                dma((width,)),
                dma((STEPS, chunks)),
                dma((STEPS, chunks)),
                dma((STEPS, chunks)),
                dma((STEPS, chunks)),
                dma((4,)),
            ] + relay,
            compiler_params=pltpu.CompilerParams(
                collective_id=0, has_side_effects=True, vmem_limit_bytes=55 * 1024 * 1024
            ),
            cost_estimate=pl.CostEstimate(
                flops=250 * STEPS * width * depth * lanes, bytes_accessed=4 * pops.size, transcendentals=0
            ),
        )(pops, heights)
        return pl.pallas_call(
            functools.partial(last_kernel, rows),
            out_shape=jax.ShapeDtypeStruct(pops.shape, pops.dtype),
            in_specs=[vmem] * 3,
            out_specs=hbm,
            scratch_shapes=[
                pltpu.VMEM((kinds, min(width, 2), depth, lanes), jnp.float32),
                dma((width,)),
                dma((chunks, 2)),
            ],
            compiler_params=pltpu.CompilerParams(vmem_limit_bytes=32 * 1024 * 1024),
            cost_estimate=pl.CostEstimate(flops=20 * pops.size, bytes_accessed=4 * pops.size, transcendentals=0),
        )(*kept)

    return jax.shard_map(
        per_device,
        mesh=mesh,
        in_specs=(P(None, ("dir", "gx"), None, None), P(("dir", "gx"), None)),
        out_specs=P(None, ("dir", "gx"), None, None),
        check_vma=False,
    )
```

```python
import functools

import jax
import jax.numpy as jnp
from jax import lax
from jax.experimental import pallas as pl
from jax.experimental.pallas import tpu as pltpu
from jax.sharding import PartitionSpec as P

STEPS = 6
PAD = 8
MESH = pl.DeviceIdType.MESH

velocity_table = [
    (0, 0, 0),
    (1, 0, 0),
    (-1, 0, 0),
    (0, 1, 0),
    (0, -1, 0),
    (0, 0, 1),
    (0, 0, -1),
    (1, 1, 0),
    (-1, -1, 0),
    (1, -1, 0),
    (-1, 1, 0),
    (1, 0, 1),
    (-1, 0, -1),
    (1, 0, -1),
    (-1, 0, 1),
    (0, 1, 1),
    (0, -1, -1),
    (0, 1, -1),
    (0, -1, 1),
]
omega_rate = 1.9
held_order = [1, 7, 9, 11, 13, 2, 8, 10, 12, 14, 0, 3, 4, 5, 6, 15, 16, 17, 18]
spot = {component: place for place, component in enumerate(held_order)}
MOVING = 5


def opposite(component):
    if component == 0:
        return 0
    return component + 1 if component % 2 == 1 else component - 1


def collide(g):
    sums = {i: g[i] + g[i + 1] for i in range(1, 19, 2)}
    diffs = {i: g[i] - g[i + 1] for i in range(1, 19, 2)}
    axis_sum = sums[1] + sums[3] + sums[5]
    cross_sum = (sums[7] + sums[9]) + (sums[11] + sums[13]) + (sums[15] + sums[17])
    total = 12.0 * g[0] + 2.0 * axis_sum + cross_sum
    scale = 3.0 * omega_rate / 36.0
    nx = scale * (2.0 * diffs[1] + ((diffs[7] + diffs[9]) + (diffs[11] + diffs[13])))
    ny = scale * (2.0 * diffs[3] + ((diffs[7] - diffs[9]) + (diffs[15] + diffs[17])))
    nz = scale * (2.0 * diffs[5] + ((diffs[11] - diffs[13]) + (diffs[15] - diffs[17])))
    k = (omega_rate * 4.5 / 36.0 / (scale * scale)) / total
    base = (omega_rate / 36.0) * total - (k * (1.0 / 3.0)) * (nx * nx + ny * ny + nz * nz)
    along = {1: nx, 3: ny, 5: nz, 7: nx + ny, 9: nx - ny, 11: nx + nz, 13: nx - nz, 15: ny + nz, 17: ny - nz}
    keep = 1.0 - omega_rate
    post = {0: base + keep * g[0]}
    for i, t in along.items():
        even = base + k * (t * t)
        post[i] = (even + t) + keep * g[i]
        post[i + 1] = (even - t) + keep * g[i + 1]
    return post


def stream(walls, rows, depth, held, plane, first):
    lanes = held.shape[-1]
    z = lax.broadcasted_iota(jnp.int32, (rows, lanes), 0) + first
    source_z = {0: z, 1: z - 1, -1: jnp.where(z == depth - 1, -1, z + 1)}
    here = pl.ds(pl.multiple_of(PAD + first, 8), rows)
    post = {i: held[spot[i], plane, here, :] for i in range(19)}
    g = {}
    for i in range(19):
        cx, cy, cz = velocity_table[i]
        if cx == 0 and cz == 0:
            moved = post[i]
        elif cz == 0:
            moved = held[spot[i], plane - cx, here, :]
        else:
            moved = held[spot[i], plane - cx, pl.ds(PAD + first - cz, rows), :]
        if cy != 0:
            moved = pltpu.roll(moved, cy % lanes, 1)
        fluid = source_z[cz] >= walls[1 + cy, plane - cx]
        g[i] = jnp.where(fluid, moved, post[opposite(i)])
    return g


def kernel(n, rows, pops, heights, last_post, walls, stage, other_post, ground, ground_sem, in_sem, sent_up, sent_down, got_up, got_down, wall_sem,
           out_up, out_down, land_up, land_down):
    width, depth, lanes = pops.shape[1], pops.shape[2], pops.shape[3]
    chunks = depth // rows
    even_post, odd_post = (other_post, last_post) if STEPS % 2 == 0 else (last_post, other_post)
    me = lax.axis_index("gx")
    right, left = lax.rem(me + 1, n), lax.rem(me + n - 1, n)
    edges = [1, width] if width > 1 else [1]
    inner = list(range(2, width))

    fetches = {
        plane: pltpu.make_async_copy(pops.at[:, plane - 1], stage.at[:, plane - 1], in_sem.at[plane - 1])
        for plane in edges + inner
    }
    for plane in edges:
        fetches[plane].start()
    ground_fetch = pltpu.make_async_copy(heights, ground, ground_sem)
    ground_fetch.start()

    barrier = pltpu.get_barrier_semaphore()
    for neighbour in (left, right):
        pl.semaphore_signal(barrier, inc=1, device_id={"gx": neighbour}, device_id_type=MESH)

    wall_up = pltpu.make_async_remote_copy(
        walls.at[1, width], walls.at[1, 0], wall_sem.at[0], wall_sem.at[1], device_id={"gx": right}, device_id_type=MESH)
    wall_down = pltpu.make_async_remote_copy(
        walls.at[1, 1], walls.at[1, width + 1], wall_sem.at[2], wall_sem.at[3], device_id={"gx": left}, device_id_type=MESH)

    def copies(step, chunk):
        up = pltpu.make_async_remote_copy(
            out_up.at[step, chunk], land_up.at[step, chunk],
            sent_up.at[step, chunk], got_up.at[step, chunk], device_id={"gx": right}, device_id_type=MESH)
        down = pltpu.make_async_remote_copy(
            out_down.at[step, chunk], land_down.at[step, chunk],
            sent_down.at[step, chunk], got_down.at[step, chunk], device_id={"gx": left}, device_id_type=MESH)
        return up, down

    def arrived(held, step, chunk):
        for copy in copies(step, chunk):
            copy.wait_recv()
        span = pl.ds(pl.multiple_of(PAD + chunk * rows, 8), rows)
        from_left, from_right = land_up[step, chunk], land_down[step, chunk]
        held[pl.ds(0, MOVING), 0, span, :] = from_left
        held[pl.ds(MOVING, MOVING), width + 1, span, :] = from_right

    def left_here(step, chunk):
        for copy in copies(step, chunk):
            copy.wait_send()

    def send(step, chunk, posts):
        for place in range(MOVING):
            out_up[step, chunk, place] = posts[width][held_order[place]]
            out_down[step, chunk, place] = posts[1][held_order[MOVING + place]]
        for copy in copies(step, chunk):
            copy.start()

    def keep_post(held, first, posts):
        span = pl.ds(pl.multiple_of(PAD + first, 8), rows)
        for plane, post in posts.items():
            for i in range(19):
                held[spot[i], plane, span, :] = post[i]

    stream_here = functools.partial(stream, walls, rows, depth)

    def first_post(planes, chunk):
        first = chunk * rows
        span = pl.ds(pl.multiple_of(first, 8), rows)
        posts = {plane: collide({i: stage[i, plane - 1, span, :] for i in range(19)}) for plane in planes}
        keep_post(even_post, first, posts)
        return posts

    for plane in edges:
        fetches[plane].wait()
    for plane in inner:
        fetches[plane].start()
    posts = first_post(edges, 0)
    pl.semaphore_wait(barrier, 2)
    send(0, 0, posts)
    ground_fetch.wait()
    for plane in range(1, width + 1):
        walls[1, plane] = jnp.broadcast_to(ground[plane - 1 : plane, :], (rows, lanes))
    wall_up.start()
    wall_down.start()

    def first_chunk(chunk, carry):
        send(0, chunk, first_post(edges, chunk))
        return carry

    lax.fori_loop(1, chunks, first_chunk, 0)
    for plane in inner:
        fetches[plane].wait()

    def first_inner(chunk, carry):
        first_post(inner, chunk)
        return carry

    lax.fori_loop(0, chunks, first_inner, 0)

    wall_up.wait()
    wall_down.wait()
    for plane in range(width + 2):
        for cy in (1, -1):
            walls[1 + cy, plane] = pltpu.roll(walls[1, plane], cy % lanes, 1)

    def one_step(step, before, held):
        arrived(before, step - 1, 0)

        def one_chunk(chunk, inside):
            first = chunk * rows

            @pl.when(chunk < chunks - 1)
            def _():
                arrived(before, step - 1, chunk + 1)

            posts = {plane: collide(stream_here(before, plane, first)) for plane in edges}
            send(step, chunk, posts)
            keep_post(held, first, posts)
            keep_post(held, first, {plane: collide(stream_here(before, plane, first)) for plane in inner})
            left_here(step - 1, chunk)
            return inside

        lax.fori_loop(0, chunks, one_chunk, 0)

    def two_steps(pair, carry):
        one_step(2 * pair + 1, even_post, odd_post)
        one_step(2 * pair + 2, odd_post, even_post)
        return carry

    lax.fori_loop(0, (STEPS - 1) // 2, two_steps, 0)
    if STEPS % 2 == 0:
        one_step(STEPS - 1, even_post, odd_post)

    def last_inner(chunk, carry):
        first = chunk * rows
        span = pl.ds(pl.multiple_of(first, 8), rows)
        streamed = {plane: stream_here(last_post, plane, first) for plane in inner}
        for plane, g in streamed.items():
            for i in range(19):
                stage[i, plane - 1, span, :] = g[i]
        return carry

    lax.fori_loop(0, chunks, last_inner, 0)

    def finish(chunk, carry):
        left_here(STEPS - 1, chunk)
        arrived(last_post, STEPS - 1, chunk)
        return carry

    lax.fori_loop(0, chunks, finish, 0)


def last_kernel(rows, last_post, walls, stage, out, ends, inner_sem, out_sem):
    width, depth = stage.shape[1], stage.shape[2]
    chunks = depth // rows
    edges = [1, width] if width > 1 else [1]
    inner_copies = [
        pltpu.make_async_copy(stage.at[:, plane - 1], out.at[:, plane - 1], inner_sem.at[plane - 1])
        for plane in range(2, width)
    ]
    for copy in inner_copies:
        copy.start()

    def write_back(chunk):
        span = pl.ds(pl.multiple_of(chunk * rows, 8), rows)
        return [
            pltpu.make_async_copy(ends.at[:, place, span], out.at[:, plane - 1, span], out_sem.at[chunk, place])
            for place, plane in enumerate(edges)
        ]

    def one_chunk(chunk, carry):
        first = chunk * rows
        span = pl.ds(pl.multiple_of(first, 8), rows)
        streamed = [stream(walls, rows, depth, last_post, plane, first) for plane in edges]
        for place, g in enumerate(streamed):
            for i in range(19):
                ends[i, place, span, :] = g[i]
        for copy in write_back(chunk):
            copy.start()
        return carry

    lax.fori_loop(0, chunks, one_chunk, 0)

    def finish(chunk, carry):
        for copy in write_back(chunk):
            copy.wait()
        return carry

    lax.fori_loop(0, chunks, finish, 0)
    for copy in inner_copies:
        copy.wait()


def solution(mesh):
    n = mesh.shape["gx"]

    def per_device(pops, heights):
        kinds, width, depth, lanes = pops.shape
        rows = 8
        chunks = depth // rows
        dma = pltpu.SemaphoreType.DMA
        held_shape = (kinds, width + 2, depth + 2 * PAD, lanes)
        wall_shape = (3, width + 2, rows, lanes)
        hbm, vmem = pl.BlockSpec(memory_space=pltpu.HBM), pl.BlockSpec(memory_space=pltpu.VMEM)
        kept = pl.pallas_call(
            functools.partial(kernel, n, rows),
            out_shape=[
                pltpu.VMEM(held_shape, jnp.float32),
                pltpu.VMEM(wall_shape, jnp.int32),
                pltpu.VMEM(pops.shape, jnp.float32),
            ],
            in_specs=[hbm] * 2,
            out_specs=[vmem] * 3,
            scratch_shapes=[
                pltpu.VMEM(held_shape, jnp.float32),
                pltpu.VMEM(heights.shape, jnp.int32),
                dma,
                dma((width,)),
                dma((STEPS, chunks)),
                dma((STEPS, chunks)),
                dma((STEPS, chunks)),
                dma((STEPS, chunks)),
                dma((4,)),
            ]
            + [pltpu.VMEM((STEPS, chunks, MOVING, rows, lanes), jnp.float32)] * 4,
            compiler_params=pltpu.CompilerParams(
                collective_id=0, has_side_effects=True, vmem_limit_bytes=55 * 1024 * 1024
            ),
            cost_estimate=pl.CostEstimate(
                flops=250 * STEPS * width * depth * lanes, bytes_accessed=4 * pops.size, transcendentals=0
            ),
        )(pops, heights)
        return pl.pallas_call(
            functools.partial(last_kernel, rows),
            out_shape=jax.ShapeDtypeStruct(pops.shape, pops.dtype),
            in_specs=[vmem] * 3,
            out_specs=hbm,
            scratch_shapes=[
                pltpu.VMEM((kinds, min(width, 2), depth, lanes), jnp.float32),
                dma((width,)),
                dma((chunks, 2)),
            ],
            compiler_params=pltpu.CompilerParams(vmem_limit_bytes=32 * 1024 * 1024),
            cost_estimate=pl.CostEstimate(flops=20 * pops.size, bytes_accessed=4 * pops.size, transcendentals=0),
        )(*kept)

    return jax.shard_map(
        per_device,
        mesh=mesh,
        in_specs=(P(None, ("dir", "gx"), None, None), P(("dir", "gx"), None)),
        out_specs=P(None, ("dir", "gx"), None, None),
        check_vma=False,
    )
```

```python
import functools

import jax
import jax.numpy as jnp
from jax import lax
from jax.experimental import pallas as pl
from jax.experimental.pallas import tpu as pltpu
from jax.sharding import PartitionSpec as P

STEPS = 6
PAD = 8
MESH = pl.DeviceIdType.MESH

velocity_table = [
    (0, 0, 0),
    (1, 0, 0),
    (-1, 0, 0),
    (0, 1, 0),
    (0, -1, 0),
    (0, 0, 1),
    (0, 0, -1),
    (1, 1, 0),
    (-1, -1, 0),
    (1, -1, 0),
    (-1, 1, 0),
    (1, 0, 1),
    (-1, 0, -1),
    (1, 0, -1),
    (-1, 0, 1),
    (0, 1, 1),
    (0, -1, -1),
    (0, 1, -1),
    (0, -1, 1),
]
omega_rate = 1.9
held_order = [1, 7, 9, 11, 13, 2, 8, 10, 12, 14, 0, 3, 4, 5, 6, 15, 16, 17, 18]
spot = {component: place for place, component in enumerate(held_order)}
MOVING = 5


def opposite(component):
    if component == 0:
        return 0
    return component + 1 if component % 2 == 1 else component - 1


def collide(g):
    sums = {i: g[i] + g[i + 1] for i in range(1, 19, 2)}
    diffs = {i: g[i] - g[i + 1] for i in range(1, 19, 2)}
    axis_sum = sums[1] + sums[3] + sums[5]
    cross_sum = (sums[7] + sums[9]) + (sums[11] + sums[13]) + (sums[15] + sums[17])
    total = 12.0 * g[0] + 2.0 * axis_sum + cross_sum
    scale = 3.0 * omega_rate / 36.0
    nx = scale * (2.0 * diffs[1] + ((diffs[7] + diffs[9]) + (diffs[11] + diffs[13])))
    ny = scale * (2.0 * diffs[3] + ((diffs[7] - diffs[9]) + (diffs[15] + diffs[17])))
    nz = scale * (2.0 * diffs[5] + ((diffs[11] - diffs[13]) + (diffs[15] - diffs[17])))
    k = (omega_rate * 4.5 / 36.0 / (scale * scale)) / total
    base = (omega_rate / 36.0) * total - (k * (1.0 / 3.0)) * (nx * nx + ny * ny + nz * nz)
    along = {1: nx, 3: ny, 5: nz, 7: nx + ny, 9: nx - ny, 11: nx + nz, 13: nx - nz, 15: ny + nz, 17: ny - nz}
    keep = 1.0 - omega_rate
    post = {0: base + keep * g[0]}
    for i, t in along.items():
        even = base + k * (t * t)
        post[i] = (even + t) + keep * g[i]
        post[i + 1] = (even - t) + keep * g[i + 1]
    return post


def stream(walls, rows, depth, held, plane, first):
    lanes = held.shape[-1]
    z = lax.broadcasted_iota(jnp.int32, (rows, lanes), 0) + first
    source_z = {0: z, 1: z - 1, -1: jnp.where(z == depth - 1, -1, z + 1)}
    here = pl.ds(pl.multiple_of(PAD + first, 8), rows)
    post = {i: held[spot[i], plane, here, :] for i in range(19)}
    g = {}
    for i in range(19):
        cx, cy, cz = velocity_table[i]
        if cx == 0 and cz == 0:
            moved = post[i]
        elif cz == 0:
            moved = held[spot[i], plane - cx, here, :]
        else:
            moved = held[spot[i], plane - cx, pl.ds(PAD + first - cz, rows), :]
        if cy != 0:
            moved = pltpu.roll(moved, cy % lanes, 1)
        fluid = source_z[cz] >= walls[1 + cy, plane - cx]
        g[i] = jnp.where(fluid, moved, post[opposite(i)])
    return g


def kernel(n, rows, pops, heights, last_post, walls, stage, other_post, ground, ground_sem, in_sem, sent_up, sent_down, got_up, got_down, wall_sem):
    width, depth, lanes = pops.shape[1], pops.shape[2], pops.shape[3]
    chunks = depth // rows
    even_post, odd_post = (other_post, last_post) if STEPS % 2 == 0 else (last_post, other_post)
    me = lax.axis_index("gx")
    right, left = lax.rem(me + 1, n), lax.rem(me + n - 1, n)
    edges = [1, width] if width > 1 else [1]
    inner = list(range(2, width))

    fetches = {
        plane: pltpu.make_async_copy(pops.at[:, plane - 1], stage.at[:, plane - 1], in_sem.at[plane - 1])
        for plane in edges + inner
    }
    for plane in edges:
        fetches[plane].start()
    ground_fetch = pltpu.make_async_copy(heights, ground, ground_sem)
    ground_fetch.start()

    barrier = pltpu.get_barrier_semaphore()
    for neighbour in (left, right):
        pl.semaphore_signal(barrier, inc=1, device_id={"gx": neighbour}, device_id_type=MESH)

    wall_up = pltpu.make_async_remote_copy(
        walls.at[1, width], walls.at[1, 0], wall_sem.at[0], wall_sem.at[1], device_id={"gx": right}, device_id_type=MESH)
    wall_down = pltpu.make_async_remote_copy(
        walls.at[1, 1], walls.at[1, width + 1], wall_sem.at[2], wall_sem.at[3], device_id={"gx": left}, device_id_type=MESH)

    def copies(held, step, chunk):
        span = pl.ds(pl.multiple_of(PAD + chunk * rows, 8), rows)
        up = pltpu.make_async_remote_copy(
            held.at[pl.ds(0, MOVING), width, span], held.at[pl.ds(0, MOVING), 0, span],
            sent_up.at[step, chunk], got_up.at[step, chunk], device_id={"gx": right}, device_id_type=MESH)
        down = pltpu.make_async_remote_copy(
            held.at[pl.ds(MOVING, MOVING), 1, span], held.at[pl.ds(MOVING, MOVING), width + 1, span],
            sent_down.at[step, chunk], got_down.at[step, chunk], device_id={"gx": left}, device_id_type=MESH)
        return up, down

    def arrived(held, step, chunk):
        for copy in copies(held, step, chunk):
            copy.wait_recv()

    def left_here(held, step, chunk):
        for copy in copies(held, step, chunk):
            copy.wait_send()

    def keep_post(held, first, posts):
        span = pl.ds(pl.multiple_of(PAD + first, 8), rows)
        for plane, post in posts.items():
            for i in range(19):
                held[spot[i], plane, span, :] = post[i]

    stream_here = functools.partial(stream, walls, rows, depth)

    def first_post(planes, chunk):
        first = chunk * rows
        span = pl.ds(pl.multiple_of(first, 8), rows)
        keep_post(even_post, first, {
            plane: collide({i: stage[i, plane - 1, span, :] for i in range(19)}) for plane in planes
        })

    for plane in edges:
        fetches[plane].wait()
    for plane in inner:
        fetches[plane].start()
    first_post(edges, 0)
    pl.semaphore_wait(barrier, 2)
    for copy in copies(even_post, 0, 0):
        copy.start()
    ground_fetch.wait()
    for plane in range(1, width + 1):
        walls[1, plane] = jnp.broadcast_to(ground[plane - 1 : plane, :], (rows, lanes))
    wall_up.start()
    wall_down.start()

    def first_chunk(chunk, carry):
        first_post(edges, chunk)
        for copy in copies(even_post, 0, chunk):
            copy.start()
        return carry

    lax.fori_loop(1, chunks, first_chunk, 0)
    for plane in inner:
        fetches[plane].wait()

    def first_inner(chunk, carry):
        first_post(inner, chunk)
        return carry

    lax.fori_loop(0, chunks, first_inner, 0)

    wall_up.wait()
    wall_down.wait()
    for plane in range(width + 2):
        for cy in (1, -1):
            walls[1 + cy, plane] = pltpu.roll(walls[1, plane], cy % lanes, 1)

    def one_step(step, before, held):
        arrived(before, step - 1, 0)

        def one_chunk(chunk, inside):
            first = chunk * rows

            sides = ((1, 0, 1), (width, 1, 0))
            for plane, needed, sent in sides:

                @pl.when(chunk < chunks - 1)
                def _():
                    copies(before, step - 1, chunk + 1)[needed].wait_recv()
                    if width == 1:
                        copies(before, step - 1, chunk + 1)[1 - needed].wait_recv()

                keep_post(held, first, {plane: collide(stream_here(before, plane, first))})
                if width == 1:
                    for copy in copies(held, step, chunk):
                        copy.start()
                    break
                copies(held, step, chunk)[sent].start()
            keep_post(held, first, {plane: collide(stream_here(before, plane, first)) for plane in inner})
            left_here(before, step - 1, chunk)
            return inside

        lax.fori_loop(0, chunks, one_chunk, 0)

    def two_steps(pair, carry):
        one_step(2 * pair + 1, even_post, odd_post)
        one_step(2 * pair + 2, odd_post, even_post)
        return carry

    lax.fori_loop(0, (STEPS - 1) // 2, two_steps, 0)
    if STEPS % 2 == 0:
        one_step(STEPS - 1, even_post, odd_post)

    def last_inner(chunk, carry):
        first = chunk * rows
        span = pl.ds(pl.multiple_of(first, 8), rows)
        streamed = {plane: stream_here(last_post, plane, first) for plane in inner}
        for plane, g in streamed.items():
            for i in range(19):
                stage[i, plane - 1, span, :] = g[i]
        return carry

    lax.fori_loop(0, chunks, last_inner, 0)

    def finish(chunk, carry):
        left_here(last_post, STEPS - 1, chunk)
        arrived(last_post, STEPS - 1, chunk)
        return carry

    lax.fori_loop(0, chunks, finish, 0)


def last_kernel(rows, last_post, walls, stage, out, ends, inner_sem, out_sem):
    width, depth = stage.shape[1], stage.shape[2]
    chunks = depth // rows
    edges = [1, width] if width > 1 else [1]
    inner_copies = [
        pltpu.make_async_copy(stage.at[:, plane - 1], out.at[:, plane - 1], inner_sem.at[plane - 1])
        for plane in range(2, width)
    ]
    for copy in inner_copies:
        copy.start()

    def write_back(chunk):
        span = pl.ds(pl.multiple_of(chunk * rows, 8), rows)
        return [
            pltpu.make_async_copy(ends.at[:, place, span], out.at[:, plane - 1, span], out_sem.at[chunk, place])
            for place, plane in enumerate(edges)
        ]

    def one_chunk(chunk, carry):
        first = chunk * rows
        span = pl.ds(pl.multiple_of(first, 8), rows)
        streamed = [stream(walls, rows, depth, last_post, plane, first) for plane in edges]
        for place, g in enumerate(streamed):
            for i in range(19):
                ends[i, place, span, :] = g[i]
        for copy in write_back(chunk):
            copy.start()
        return carry

    lax.fori_loop(0, chunks, one_chunk, 0)

    def finish(chunk, carry):
        for copy in write_back(chunk):
            copy.wait()
        return carry

    lax.fori_loop(0, chunks, finish, 0)
    for copy in inner_copies:
        copy.wait()


def solution(mesh):
    n = mesh.shape["gx"]

    def per_device(pops, heights):
        kinds, width, depth, lanes = pops.shape
        rows = 8
        chunks = depth // rows
        dma = pltpu.SemaphoreType.DMA
        held_shape = (kinds, width + 2, depth + 2 * PAD, lanes)
        wall_shape = (3, width + 2, rows, lanes)
        hbm, vmem = pl.BlockSpec(memory_space=pltpu.HBM), pl.BlockSpec(memory_space=pltpu.VMEM)
        kept = pl.pallas_call(
            functools.partial(kernel, n, rows),
            out_shape=[
                pltpu.VMEM(held_shape, jnp.float32),
                pltpu.VMEM(wall_shape, jnp.int32),
                pltpu.VMEM(pops.shape, jnp.float32),
            ],
            in_specs=[hbm] * 2,
            out_specs=[vmem] * 3,
            scratch_shapes=[
                pltpu.VMEM(held_shape, jnp.float32),
                pltpu.VMEM(heights.shape, jnp.int32),
                dma,
                dma((width,)),
                dma((STEPS, chunks)),
                dma((STEPS, chunks)),
                dma((STEPS, chunks)),
                dma((STEPS, chunks)),
                dma((4,)),
            ],
            compiler_params=pltpu.CompilerParams(
                collective_id=0, has_side_effects=True, vmem_limit_bytes=55 * 1024 * 1024
            ),
            cost_estimate=pl.CostEstimate(
                flops=250 * STEPS * width * depth * lanes, bytes_accessed=4 * pops.size, transcendentals=0
            ),
        )(pops, heights)
        return pl.pallas_call(
            functools.partial(last_kernel, rows),
            out_shape=jax.ShapeDtypeStruct(pops.shape, pops.dtype),
            in_specs=[vmem] * 3,
            out_specs=hbm,
            scratch_shapes=[
                pltpu.VMEM((kinds, min(width, 2), depth, lanes), jnp.float32),
                dma((width,)),
                dma((chunks, 2)),
            ],
            compiler_params=pltpu.CompilerParams(vmem_limit_bytes=32 * 1024 * 1024),
            cost_estimate=pl.CostEstimate(flops=20 * pops.size, bytes_accessed=4 * pops.size, transcendentals=0),
        )(*kept)

    return jax.shard_map(
        per_device,
        mesh=mesh,
        in_specs=(P(None, ("dir", "gx"), None, None), P(("dir", "gx"), None)),
        out_specs=P(None, ("dir", "gx"), None, None),
        check_vma=False,
    )
```

```python
import functools

import jax
import jax.numpy as jnp
from jax import lax
from jax.experimental import pallas as pl
from jax.experimental.pallas import tpu as pltpu
from jax.sharding import PartitionSpec as P

STEPS = 6
PAD = 8
MESH = pl.DeviceIdType.MESH

velocity_table = [
    (0, 0, 0),
    (1, 0, 0),
    (-1, 0, 0),
    (0, 1, 0),
    (0, -1, 0),
    (0, 0, 1),
    (0, 0, -1),
    (1, 1, 0),
    (-1, -1, 0),
    (1, -1, 0),
    (-1, 1, 0),
    (1, 0, 1),
    (-1, 0, -1),
    (1, 0, -1),
    (-1, 0, 1),
    (0, 1, 1),
    (0, -1, -1),
    (0, 1, -1),
    (0, -1, 1),
]
omega_rate = 1.9
held_order = [1, 7, 9, 11, 13, 2, 8, 10, 12, 14, 0, 3, 4, 5, 6, 15, 16, 17, 18]
spot = {component: place for place, component in enumerate(held_order)}
MOVING = 5


def opposite(component):
    if component == 0:
        return 0
    return component + 1 if component % 2 == 1 else component - 1


def collide(g):
    sums = {i: g[i] + g[i + 1] for i in range(1, 19, 2)}
    diffs = {i: g[i] - g[i + 1] for i in range(1, 19, 2)}
    axis_sum = sums[1] + sums[3] + sums[5]
    cross_sum = (sums[7] + sums[9]) + (sums[11] + sums[13]) + (sums[15] + sums[17])
    total = 12.0 * g[0] + 2.0 * axis_sum + cross_sum
    scale = 3.0 * omega_rate / 36.0
    nx = scale * (2.0 * diffs[1] + ((diffs[7] + diffs[9]) + (diffs[11] + diffs[13])))
    ny = scale * (2.0 * diffs[3] + ((diffs[7] - diffs[9]) + (diffs[15] + diffs[17])))
    nz = scale * (2.0 * diffs[5] + ((diffs[11] - diffs[13]) + (diffs[15] - diffs[17])))
    k = (omega_rate * 4.5 / 36.0 / (scale * scale)) / total
    base = (omega_rate / 36.0) * total - (k * (1.0 / 3.0)) * (nx * nx + ny * ny + nz * nz)
    along = {1: nx, 3: ny, 5: nz, 7: nx + ny, 9: nx - ny, 11: nx + nz, 13: nx - nz, 15: ny + nz, 17: ny - nz}
    keep = 1.0 - omega_rate
    post = {0: base + keep * g[0]}
    for i, t in along.items():
        even = base + k * (t * t)
        post[i] = (even + t) + keep * g[i]
        post[i + 1] = (even - t) + keep * g[i + 1]
    return post


def stream(walls, rows, depth, held, plane, first):
    lanes = held.shape[-1]
    z = lax.broadcasted_iota(jnp.int32, (rows, lanes), 0) + first
    source_z = {0: z, 1: z - 1, -1: jnp.where(z == depth - 1, -1, z + 1)}
    here = pl.ds(pl.multiple_of(PAD + first, 8), rows)
    post = {i: held[spot[i], plane, here, :] for i in range(19)}
    g = {}
    for i in range(19):
        cx, cy, cz = velocity_table[i]
        if cx == 0 and cz == 0:
            moved = post[i]
        elif cz == 0:
            moved = held[spot[i], plane - cx, here, :]
        else:
            moved = held[spot[i], plane - cx, pl.ds(PAD + first - cz, rows), :]
        if cy != 0:
            moved = pltpu.roll(moved, cy % lanes, 1)
        fluid = source_z[cz] >= walls[1 + cy, plane - cx]
        g[i] = jnp.where(fluid, moved, post[opposite(i)])
    return g


def kernel(n, rows, pops, heights, last_post, walls, stage, other_post, ground, ground_sem, in_sem, sent_up, sent_down, got_up, got_down, wall_sem):
    width, depth, lanes = pops.shape[1], pops.shape[2], pops.shape[3]
    chunks = depth // rows
    even_post, odd_post = (other_post, last_post) if STEPS % 2 == 0 else (last_post, other_post)
    me = lax.axis_index("gx")
    right, left = lax.rem(me + 1, n), lax.rem(me + n - 1, n)
    edges = [1, width] if width > 1 else [1]
    inner = list(range(2, width))

    fetches = {
        plane: pltpu.make_async_copy(pops.at[:, plane - 1], stage.at[:, plane - 1], in_sem.at[plane - 1])
        for plane in edges + inner
    }
    for plane in edges:
        fetches[plane].start()
    ground_fetch = pltpu.make_async_copy(heights, ground, ground_sem)
    ground_fetch.start()

    barrier = pltpu.get_barrier_semaphore()
    for neighbour in (left, right):
        pl.semaphore_signal(barrier, inc=1, device_id={"gx": neighbour}, device_id_type=MESH)

    wall_up = pltpu.make_async_remote_copy(
        walls.at[1, width], walls.at[1, 0], wall_sem.at[0], wall_sem.at[1], device_id={"gx": right}, device_id_type=MESH)
    wall_down = pltpu.make_async_remote_copy(
        walls.at[1, 1], walls.at[1, width + 1], wall_sem.at[2], wall_sem.at[3], device_id={"gx": left}, device_id_type=MESH)

    def copies(held, step, chunk):
        span = pl.ds(pl.multiple_of(PAD + chunk * rows, 8), rows)
        up = pltpu.make_async_remote_copy(
            held.at[pl.ds(0, MOVING), width, span], held.at[pl.ds(0, MOVING), 0, span],
            sent_up.at[step, chunk], got_up.at[step, chunk], device_id={"gx": right}, device_id_type=MESH)
        down = pltpu.make_async_remote_copy(
            held.at[pl.ds(MOVING, MOVING), 1, span], held.at[pl.ds(MOVING, MOVING), width + 1, span],
            sent_down.at[step, chunk], got_down.at[step, chunk], device_id={"gx": left}, device_id_type=MESH)
        return up, down

    def arrived(held, step, chunk):
        for copy in copies(held, step, chunk):
            copy.wait_recv()

    def left_here(held, step, chunk):
        for copy in copies(held, step, chunk):
            copy.wait_send()

    def keep_post(held, first, posts):
        span = pl.ds(pl.multiple_of(PAD + first, 8), rows)
        for plane, post in posts.items():
            for i in range(19):
                held[spot[i], plane, span, :] = post[i]

    stream_here = functools.partial(stream, walls, rows, depth)

    def first_post(planes, chunk):
        first = chunk * rows
        span = pl.ds(pl.multiple_of(first, 8), rows)
        keep_post(even_post, first, {
            plane: collide({i: stage[i, plane - 1, span, :] for i in range(19)}) for plane in planes
        })

    for plane in edges:
        fetches[plane].wait()
    for plane in inner:
        fetches[plane].start()
    first_post(edges, 0)
    pl.semaphore_wait(barrier, 2)
    for copy in copies(even_post, 0, 0):
        copy.start()
    ground_fetch.wait()
    for plane in range(1, width + 1):
        walls[1, plane] = jnp.broadcast_to(ground[plane - 1 : plane, :], (rows, lanes))
    wall_up.start()
    wall_down.start()

    def first_chunk(chunk, carry):
        first_post(edges, chunk)
        for copy in copies(even_post, 0, chunk):
            copy.start()
        return carry

    lax.fori_loop(1, chunks, first_chunk, 0)
    for plane in inner:
        fetches[plane].wait()

    def first_inner(chunk, carry):
        first_post(inner, chunk)
        return carry

    lax.fori_loop(0, chunks, first_inner, 0)

    wall_up.wait()
    wall_down.wait()
    for plane in range(width + 2):
        for cy in (1, -1):
            walls[1 + cy, plane] = pltpu.roll(walls[1, plane], cy % lanes, 1)

    def one_step(step, before, held):
        arrived(before, step - 1, 0)

        def one_chunk(chunk, inside):
            first = chunk * rows

            @pl.when(chunk < chunks - 1)
            def _():
                arrived(before, step - 1, chunk + 1)

            keep_post(held, first, {plane: collide(stream_here(before, plane, first)) for plane in edges})
            for copy in copies(held, step, chunk):
                copy.start()
            keep_post(held, first, {plane: collide(stream_here(before, plane, first)) for plane in inner})
            left_here(before, step - 1, chunk)
            return inside

        lax.fori_loop(0, chunks, one_chunk, 0)

    def two_steps(pair, carry):
        one_step(2 * pair + 1, even_post, odd_post)
        one_step(2 * pair + 2, odd_post, even_post)
        return carry

    lax.fori_loop(0, (STEPS - 1) // 2, two_steps, 0)
    if STEPS % 2 == 0:
        one_step(STEPS - 1, even_post, odd_post)

    def last_inner(chunk, carry):
        first = chunk * rows
        span = pl.ds(pl.multiple_of(first, 8), rows)
        streamed = {plane: stream_here(last_post, plane, first) for plane in inner}
        for plane, g in streamed.items():
            for i in range(19):
                stage[i, plane - 1, span, :] = g[i]
        return carry

    lax.fori_loop(0, chunks, last_inner, 0)

    def finish(chunk, carry):
        left_here(last_post, STEPS - 1, chunk)
        arrived(last_post, STEPS - 1, chunk)
        return carry

    lax.fori_loop(0, chunks, finish, 0)


def last_kernel(rows, last_post, walls, stage, out, ends, inner_sem, out_sem):
    width, depth = stage.shape[1], stage.shape[2]
    chunks = depth // rows
    edges = [1, width] if width > 1 else [1]
    inner_copies = [
        pltpu.make_async_copy(stage.at[:, plane - 1], out.at[:, plane - 1], inner_sem.at[plane - 1])
        for plane in range(2, width)
    ]
    for copy in inner_copies:
        copy.start()

    group = 4 if chunks % 4 == 0 else 1

    def write_back(chunk):
        span = pl.ds(pl.multiple_of((chunk - group + 1) * rows, 8), group * rows)
        return [
            pltpu.make_async_copy(ends.at[:, place, span], out.at[:, plane - 1, span], out_sem.at[chunk, place])
            for place, plane in enumerate(edges)
        ]

    def one_chunk(chunk, carry):
        first = chunk * rows
        span = pl.ds(pl.multiple_of(first, 8), rows)
        streamed = [stream(walls, rows, depth, last_post, plane, first) for plane in edges]
        for place, g in enumerate(streamed):
            for i in range(19):
                ends[i, place, span, :] = g[i]

        @pl.when(chunk % group == group - 1)
        def _():
            for copy in write_back(chunk):
                copy.start()

        return carry

    lax.fori_loop(0, chunks, one_chunk, 0)

    def finish(chunk, carry):
        for copy in write_back(chunk * group + group - 1):
            copy.wait()
        return carry

    lax.fori_loop(0, chunks // group, finish, 0)
    for copy in inner_copies:
        copy.wait()


def solution(mesh):
    n = mesh.shape["gx"]

    def per_device(pops, heights):
        kinds, width, depth, lanes = pops.shape
        rows = 8
        chunks = depth // rows
        dma = pltpu.SemaphoreType.DMA
        held_shape = (kinds, width + 2, depth + 2 * PAD, lanes)
        wall_shape = (3, width + 2, rows, lanes)
        hbm, vmem = pl.BlockSpec(memory_space=pltpu.HBM), pl.BlockSpec(memory_space=pltpu.VMEM)
        kept = pl.pallas_call(
            functools.partial(kernel, n, rows),
            out_shape=[
                pltpu.VMEM(held_shape, jnp.float32),
                pltpu.VMEM(wall_shape, jnp.int32),
                pltpu.VMEM(pops.shape, jnp.float32),
            ],
            in_specs=[hbm] * 2,
            out_specs=[vmem] * 3,
            scratch_shapes=[
                pltpu.VMEM(held_shape, jnp.float32),
                pltpu.VMEM(heights.shape, jnp.int32),
                dma,
                dma((width,)),
                dma((STEPS, chunks)),
                dma((STEPS, chunks)),
                dma((STEPS, chunks)),
                dma((STEPS, chunks)),
                dma((4,)),
            ],
            compiler_params=pltpu.CompilerParams(
                collective_id=0, has_side_effects=True, vmem_limit_bytes=55 * 1024 * 1024
            ),
            cost_estimate=pl.CostEstimate(
                flops=250 * STEPS * width * depth * lanes, bytes_accessed=4 * pops.size, transcendentals=0
            ),
        )(pops, heights)
        return pl.pallas_call(
            functools.partial(last_kernel, rows),
            out_shape=jax.ShapeDtypeStruct(pops.shape, pops.dtype),
            in_specs=[vmem] * 3,
            out_specs=hbm,
            scratch_shapes=[
                pltpu.VMEM((kinds, min(width, 2), depth, lanes), jnp.float32),
                dma((width,)),
                dma((chunks, 2)),
            ],
            compiler_params=pltpu.CompilerParams(vmem_limit_bytes=32 * 1024 * 1024),
            cost_estimate=pl.CostEstimate(flops=20 * pops.size, bytes_accessed=4 * pops.size, transcendentals=0),
        )(*kept)

    return jax.shard_map(
        per_device,
        mesh=mesh,
        in_specs=(P(None, ("dir", "gx"), None, None), P(("dir", "gx"), None)),
        out_specs=P(None, ("dir", "gx"), None, None),
        check_vma=False,
    )
```
